32 devices in a mesh: src: 8 (over z, core), dst: 4 (over y, x).
Axes of the slice: x: 2, y: 2, z: 4, core: 2. Of those that a mesh axis runs over, the one named last changes fastest.
Arguments:
- adjacency: float32 [5120, 5120], P('dst', 'src'), may hold values from -0.125 to 0.125
- features: float32 [5120, 256], P(('src', 'dst')), may hold values from -6 to 6
- layer_weights: float32 [2, 2, 256, 256], replicated, may hold values from -0.375 to 0.375
- layer_biases: float32 [2, 256], replicated, may hold values from -3 to 3
Outputs:
- result: float32 [5120, 256], P(('src', 'dst'))
The draws below stay inside these ranges and needn't reach their ends.
All inputs are finite; a program needn't handle non-finite values.
Results may differ from the reference program's by a relative error of at most 0.0001.
Values sent between devices are 32-bit elements; how exact they have to be, the bound alone decides.
A program may use at most 128 MiB of HBM per device.

```python
import jax
import jax.numpy as jnp
from jax import lax

F = 256
LAYERS = 2
NODES = 5120


def strengthened(array, key, source, target, shards_of, factor):
    owner, partner = [(jnp.arange(array.shape[position]) // (array.shape[position] // shards_of)).reshape([-1 if axis == position else 1 for axis in range(array.ndim)]) for position in (source, target)]
    chosen = jax.random.permutation(key, shards_of)[partner]
    strong = (owner == chosen) | (owner == (partner + shards_of // 2) % shards_of)
    return jnp.where(strong, factor * array, array)


def level_of(key, extent, split, low, high):
    gain = 1.0
    for axis_at, shards_of in split:
        heights = jax.random.uniform(jax.random.fold_in(jax.random.fold_in(key, 6), axis_at), (shards_of,), jnp.float32, low / len(split), high / len(split))
        gain = gain * jnp.repeat(jnp.exp(heights), extent[axis_at] // shards_of).reshape((-1,) + (1,) * (len(extent) - 1 - axis_at))
    return gain


def normal_values(own_key, extent, scale, reach, pieces=(), dtype=jnp.bfloat16):
    factor_of = level_of(own_key, extent, pieces, -0.22, 0.18) if pieces else 1.0
    entries = jax.random.normal(own_key, extent, jnp.float32) * scale * factor_of
    return jnp.minimum(jnp.maximum(entries, -reach), reach).astype(dtype)


def heavy_noise(own_key, dims, width, bound, split, heavy, dtype=jnp.bfloat16):
    drawn = width * jax.random.normal(own_key, dims, jnp.float32)
    if split:
        drawn = drawn * level_of(own_key, dims, split, -0.22, 0.18)
    return jnp.clip(strengthened(drawn, jax.random.fold_in(own_key, 3), *heavy), -bound, bound).astype(dtype)


def setup_inputs(seed: int = 0) -> dict:
    splits = jax.random.split(jax.random.key(seed), 5)
    return {
        "adjacency": heavy_noise(splits[0], (NODES, NODES), NODES ** -0.5, 0.125, ((0, 4), (1, 8)), (1, 0, 8, 2.0), jnp.float32),
        "features": normal_values(splits[1], (NODES, F), 1.0, 6.0, ((0, 32),), jnp.float32),
        "layer_weights": normal_values(splits[2], (LAYERS, 2, F, F), F ** -0.5, 0.375, (), jnp.float32),
        "layer_biases": normal_values(splits[3], (LAYERS, F), 0.5, 3.0, (), jnp.float32),
    }


def reference(adjacency, features, layer_weights, layer_biases):
    current = features
    for layer_index in range(LAYERS):
        forward = jnp.dot(adjacency, current, precision=lax.Precision.HIGHEST, preferred_element_type=jnp.float32)
        reverse = lax.dot_general(adjacency, current, (((0,), (0,)), ((), ())), precision=lax.Precision.HIGHEST, preferred_element_type=jnp.float32)
        mixed = jnp.dot(forward, layer_weights[layer_index, 0], precision=lax.Precision.HIGHEST, preferred_element_type=jnp.float32)
        mixed = mixed + jnp.dot(reverse, layer_weights[layer_index, 1], precision=lax.Precision.HIGHEST, preferred_element_type=jnp.float32)
        current = jax.nn.relu(mixed + layer_biases[layer_index][None, :])
    return current
```

```python
import jax
import jax.numpy as jnp
from jax import lax
from jax.sharding import PartitionSpec as P

HIGH = lax.Precision.HIGH


def matmul(a, b, dims=(((1,), (0,)), ((), ()))):
    return lax.dot_general(a, b, dims, precision=HIGH, preferred_element_type=jnp.float32)


def body(adjacency, features, layer_weights, layer_biases):
    n_src, n_dst = lax.axis_size("src"), lax.axis_size("dst")
    owner = [(g, (g % n_src) * n_dst + g // n_src) for g in range(n_src * n_dst)]
    back = [(b, a) for a, b in owner]
    rows = features
    for layer in range(layer_weights.shape[0]):
        share = lax.ppermute(rows, ("src", "dst"), owner)
        source_rows = lax.all_gather(rows, "dst", axis=0, tiled=True)
        dest_rows = lax.all_gather(share, "src", axis=0, tiled=True)
        partial_rows = matmul(adjacency, source_rows)
        forward = lax.psum_scatter(partial_rows, "src", scatter_dimension=0, tiled=True)
        forward = lax.ppermute(forward, ("src", "dst"), back)
        partial_cols = matmul(adjacency, dest_rows, (((0,), (0,)), ((), ())))
        reverse = lax.psum_scatter(partial_cols, "dst", scatter_dimension=0, tiled=True)
        mixed = matmul(forward, layer_weights[layer, 0]) + matmul(reverse, layer_weights[layer, 1])
        rows = jax.nn.relu(mixed + layer_biases[layer][None, :])
    return rows


def solution(mesh):
    placed = (P("dst", "src"), P(("src", "dst"), None), P(), P())
    return jax.shard_map(
        body, mesh=mesh, in_specs=placed, out_specs=P(("src", "dst"), None), check_vma=False
    )
```

```python
import functools

import jax
import jax.numpy as jnp
from jax import lax
from jax.experimental import pallas as pl
from jax.experimental.pallas import tpu as pltpu
from jax.sharding import PartitionSpec as P

MESH = pl.DeviceIdType.MESH
CORES = 2
SPLIT = 2


def parts_of(value):
    high = value.astype(jnp.bfloat16)
    return high, (value - high.astype(jnp.float32)).astype(jnp.bfloat16)


def dot3(a_high, a_low, b_high, b_low):
    dot = functools.partial(jnp.dot, preferred_element_type=jnp.float32)
    return dot(a_high, b_high) + (dot(a_high, b_low) + dot(a_low, b_high))


def kernel(
    n, layers, tile,
    adj, feat, weights, biases, out,
    stage, a_hi, a_lo, t_hi, t_lo, xs_hi, xs_lo,
    xs, xd, swap_out, own, rev, pair_in, chain_in, rev_in, total_in,
    load_sem, gs, gr, zs, zr, cs, cr, ps, pr, hs, hr, fs, fr, vs, vr,
):
    rows, width = feat.shape
    half = n * rows
    chunk = rows // SPLIT
    chunks = n * SPLIT
    tiles = CORES * half // tile
    s, d = lax.axis_index("src"), lax.axis_index("dst")
    u, c = lax.div(s, CORES), lax.rem(s, CORES)
    root = u == d
    below = jnp.logical_and(u <= d, u > 0)
    above = jnp.logical_and(u >= d, u < n - 1)
    distance = jnp.abs(u - d)
    reach = jnp.where(u < d, d, n - 1 - d)
    lag = jnp.where(root, 0, reach - distance)
    mate = {"src": u * CORES + 1 - c, "dst": d}
    down = {"src": s - CORES, "dst": d}
    up = {"src": s + CORES, "dst": d}
    inward = {"src": jnp.where(u < d, s + CORES, s - CORES), "dst": d}
    side = jnp.where(u < d, 0, 1)

    def peer(j):
        return {"src": s, "dst": lax.rem(d + j, n)}

    def span(start, size):
        return pl.ds(pl.multiple_of(start, size), size)

    def remote(src, dst, send, recv, device):
        return pltpu.make_async_remote_copy(
            src_ref=src, dst_ref=dst, send_sem=send, recv_sem=recv,
            device_id=device, device_id_type=MESH,
        )

    def load(t, slot):
        return pltpu.make_async_copy(adj.at[span(t * tile, tile)], stage.at[slot], load_sem.at[slot])

    load(0, 0).start()
    if tiles > 1:
        load(1, 1).start()

    barrier = pltpu.get_barrier_semaphore()
    for j in range(1, n):
        pl.semaphore_signal(barrier, inc=1, device_id=peer(j), device_id_type=MESH)
    pl.semaphore_signal(barrier, inc=1, device_id=mate, device_id_type=MESH)

    @pl.when(u > 0)
    def _():
        pl.semaphore_signal(barrier, inc=1, device_id=down, device_id_type=MESH)

    @pl.when(u < n - 1)
    def _():
        pl.semaphore_signal(barrier, inc=1, device_id=up, device_id_type=MESH)

    xs[0, span(d * rows, rows)] = feat[...]
    pl.semaphore_wait(barrier, n + (u > 0).astype(jnp.int32) + (u < n - 1).astype(jnp.int32))

    def prepare():
        def step(t, carry):
            slot = lax.rem(t, 2)
            load(t, slot).wait()
            block = stage[slot]
            high, low = parts_of(block)
            a_hi[span(t * tile, tile)] = high
            a_lo[span(t * tile, tile)] = low
            turned_high, turned_low = parts_of(block.T)
            t_hi[t] = turned_high
            t_lo[t] = turned_low

            @pl.when(t + 2 < tiles)
            def _():
                load(t + 2, slot).start()

            return carry

        lax.fori_loop(0, tiles, step, 0)

    for l in range(layers):

        def gather(j):
            own_rows = xs.at[l, span(d * rows, rows)]
            return remote(own_rows, own_rows, gs.at[l, j], gr.at[l, n - j], peer(j))

        def gathered(i):
            rows_of = xs.at[l, span(lax.rem(d + i, n) * rows, rows)]
            return remote(rows_of, rows_of, gs.at[l, i], gr.at[l, i], peer(i))

        def place(k):
            group = lax.rem(d + lax.div(k, SPLIT), n)
            return group * rows + lax.rem(k, SPLIT) * chunk

        def spread(k, to, device):
            ref = xd.at[l, span(c * half + place(k), chunk)]
            return remote(ref, ref, zs.at[l, to, k], zr.at[l, k], device)

        def share(k):
            ref = xd.at[l, span(c * half + place(k), chunk)]
            return remote(ref, ref, cs.at[l, k], cr.at[l, k], mate)

        def spread_group(g):
            for part in range(SPLIT):
                k = g * SPLIT + part

                @pl.when(root)
                def _():
                    xd[l, span(c * half + place(k), chunk)] = xs[l, span(place(k), chunk)]

                @pl.when(jnp.logical_not(root))
                def _():
                    spread(k, 0, down).wait_recv()

                @pl.when(below)
                def _():
                    spread(k, 0, down).start()

                @pl.when(above)
                def _():
                    spread(k, 1, up).start()

                share(k).start()

        def pair(k):
            span_k = span(k * chunk, chunk)
            return remote(swap_out.at[span_k], pair_in.at[l, span_k], ps.at[l, k], pr.at[l, k], mate)

        def chain(k, which):
            span_k = span(k * chunk, chunk)
            return remote(
                own.at[span_k], chain_in.at[l, which, span_k], hs.at[l, k], hr.at[l, which, k], inward
            )

        def total(r):
            return remote(
                own.at[span(r * rows, rows)], total_in.at[l], fs.at[l, r], fr.at[l], {"src": s, "dst": r}
            )

        def reduce_group(r):
            for part in range(SPLIT):
                k = r * SPLIT + part
                span_k = span(k * chunk, chunk)
                pair(k).wait_recv()
                own[span_k] = own[span_k] + pair_in[l, span_k]

                @pl.when(below)
                def _():
                    chain(k, 0).wait_recv()
                    own[span_k] = own[span_k] + chain_in[l, 0, span_k]

                @pl.when(above)
                def _():
                    chain(k, 1).wait_recv()
                    own[span_k] = own[span_k] + chain_in[l, 1, span_k]

                @pl.when(jnp.logical_not(root))
                def _():
                    chain(k, side).start()

            @pl.when(jnp.logical_and(root, r == d))
            def _():
                total_in[l] = own[span(r * rows, rows)]

            @pl.when(jnp.logical_and(root, r != d))
            def _():
                total(r).start()

        def reverse_out(j):
            rows_of = rev.at[span(lax.rem(d + j, n) * rows, rows)]
            return remote(rows_of, rev_in.at[l, n - j], vs.at[l, j], vr.at[l, n - j], peer(j))

        def reverse():
            def arrive(k, carry):
                share(k).wait_recv()
                return carry

            lax.fori_loop(0, chunks, arrive, 0)
            rev[...] = jnp.zeros_like(rev)

            def step(t, carry):
                x_hi, x_lo = parts_of(xd[l, span(t * tile, tile)])
                rev[...] += dot3(t_hi[t], t_lo[t], x_hi, x_lo)
                return carry

            lax.fori_loop(0, tiles, step, 0)
            for j in range(1, n):
                reverse_out(j).start()

        for j in range(1, n):
            gather(j).start()
        for i in range(n):
            if i > 0:
                gathered(i).wait_recv()

            @pl.when(i >= distance)
            def _():
                spread_group(i - distance)

            if l == 0 and i == 0:
                prepare()

        x_hi, x_lo = parts_of(xs[l])
        xs_hi[...] = x_hi
        xs_lo[...] = x_lo
        strip = half // 2
        strip_chunks = chunks // 2

        def forward(i, carry):
            start = i * strip
            at = span((1 - c) * half + start, strip)
            swap_out[span(start, strip)] = dot3(a_hi[at], a_lo[at], xs_hi[...], xs_lo[...])

            def post(k, inner):
                pair(i * strip_chunks + k).start()
                return inner

            lax.fori_loop(0, strip_chunks, post, 0)
            return carry

        lax.fori_loop(0, 2, forward, 0)

        def forward_own(i, carry):
            start = i * strip
            at = span(c * half + start, strip)
            own[span(start, strip)] = dot3(a_hi[at], a_lo[at], xs_hi[...], xs_lo[...])
            return carry

        lax.fori_loop(0, 2, forward_own, 0)

        def turn(t, carry):
            @pl.when(t < distance)
            def _():
                spread_group(n - distance + t)

            @pl.when(t == distance)
            def _():
                reverse()

            @pl.when(jnp.logical_and(t >= lag, t < lag + n))
            def _():
                reduce_group(t - lag)

            return carry

        lax.fori_loop(0, 2 * n - 1, turn, 0)

        back = rev[span(d * rows, rows)]
        for i in range(1, n):
            remote(
                rev.at[span(d * rows, rows)], rev_in.at[l, i], vs.at[l, i], vr.at[l, i], peer(i)
            ).wait_recv()
            back = back + rev_in[l, i]

        @pl.when(jnp.logical_not(root))
        def _():
            total(d).wait_recv()

        mixed = dot3(*parts_of(total_in[l]), *parts_of(weights[l, 0]))
        mixed = mixed + dot3(*parts_of(back), *parts_of(weights[l, 1]))
        result = jnp.maximum(mixed + biases[pl.ds(l, 1)], 0.0)
        if l + 1 < layers:
            xs[l + 1, span(d * rows, rows)] = result
        else:
            out[...] = result

        for j in range(1, n):
            gather(j).wait_send()
            reverse_out(j).wait_send()

        def drain(k, carry):
            share(k).wait_send()
            pair(k).wait_send()

            @pl.when(below)
            def _():
                spread(k, 0, down).wait_send()

            @pl.when(above)
            def _():
                spread(k, 1, up).wait_send()

            @pl.when(jnp.logical_not(root))
            def _():
                chain(k, side).wait_send()

            return carry

        lax.fori_loop(0, chunks, drain, 0)
        for r in range(n):

            @pl.when(jnp.logical_and(root, r != d))
            def _():
                total(r).wait_send()


def body(adjacency, features, layer_weights, layer_biases):
    n = lax.axis_size("dst")
    assert lax.axis_size("src") == CORES * n
    layers = layer_weights.shape[0]
    rows, width = features.shape
    half = n * rows
    tile = 256
    tiles = CORES * half // tile
    chunks = n * SPLIT
    f32, bf16 = jnp.float32, jnp.bfloat16
    dma = pltpu.SemaphoreType.DMA
    vmem = pltpu.VMEM
    scratch = [
        vmem((2, tile, half), f32),
        vmem((CORES * half, half), bf16),
        vmem((CORES * half, half), bf16),
        vmem((tiles, half, tile), bf16),
        vmem((tiles, half, tile), bf16),
        vmem((half, width), bf16),
        vmem((half, width), bf16),
        vmem((layers, half, width), f32),
        vmem((layers, CORES * half, width), f32),
        vmem((half, width), f32),
        vmem((half, width), f32),
        vmem((half, width), f32),
        vmem((layers, half, width), f32),
        vmem((layers, 2, half, width), f32),
        vmem((layers, n, rows, width), f32),
        vmem((layers, rows, width), f32),
        dma((2,)),
        dma((layers, n)),
        dma((layers, n)),
        dma((layers, 2, chunks)),
        dma((layers, chunks)),
        dma((layers, chunks)),
        dma((layers, chunks)),
        dma((layers, chunks)),
        dma((layers, chunks)),
        dma((layers, chunks)),
        dma((layers, 2, chunks)),
        dma((layers, n)),
        dma((layers,)),
        dma((layers, n)),
        dma((layers, n)),
    ]
    in_vmem = pl.BlockSpec(memory_space=pltpu.VMEM)
    flops = 2 * 3 * 2 * layers * CORES * half * half * width
    return pl.pallas_call(
        functools.partial(kernel, n, layers, tile),
        out_shape=jax.ShapeDtypeStruct((rows, width), f32),
        in_specs=[pl.BlockSpec(memory_space=pl.ANY), in_vmem, in_vmem, in_vmem],
        out_specs=in_vmem,
        scratch_shapes=scratch,
        compiler_params=pltpu.CompilerParams(
            collective_id=0, has_side_effects=True, vmem_limit_bytes=60 * 2**20
        ),
        cost_estimate=pl.CostEstimate(
            flops=flops, bytes_accessed=adjacency.size * 4, transcendentals=0
        ),
    )(adjacency, features, layer_weights, layer_biases)


def solution(mesh):
    placed = (P("dst", "src"), P(("src", "dst"), None), P(), P())
    return jax.shard_map(
        body, mesh=mesh, in_specs=placed, out_specs=P(("src", "dst"), None), check_vma=False
    )
```

```python
import functools

import jax
import jax.numpy as jnp
from jax import lax
from jax.experimental import pallas as pl
from jax.experimental.pallas import tpu as pltpu
from jax.sharding import PartitionSpec as P

MESH = pl.DeviceIdType.MESH
CORES = 2
SPLIT = 2


def parts_of(value):
    high = value.astype(jnp.bfloat16)
    return high, (value - high.astype(jnp.float32)).astype(jnp.bfloat16)


def dot3(a_high, a_low, b_high, b_low):
    dot = functools.partial(jnp.dot, preferred_element_type=jnp.float32)
    return dot(a_high, b_high) + (dot(a_high, b_low) + dot(a_low, b_high))


def kernel(
    n, layers, tile,
    adj, feat, weights, biases, out,
    stage, a_hi, a_lo, t_hi, t_lo, xs_hi, xs_lo,
    xs, xd, swap_out, own, rev, pair_in, chain_in, rev_in, total_in,
    load_sem, gs, gr, zs, zr, cs, cr, ps, pr, hs, hr, fs, fr, vs, vr,
):
    rows, width = feat.shape
    half = n * rows
    chunk = rows // SPLIT
    chunks = n * SPLIT
    tiles = CORES * half // tile
    s, d = lax.axis_index("src"), lax.axis_index("dst")
    u, c = lax.div(s, CORES), lax.rem(s, CORES)
    root = u == d
    below = jnp.logical_and(u <= d, u > 0)
    above = jnp.logical_and(u >= d, u < n - 1)
    distance = jnp.abs(u - d)
    reach = jnp.where(u < d, d, n - 1 - d)
    tip = jnp.logical_and(jnp.logical_not(root), distance == reach)
    lag = jnp.where(jnp.logical_or(root, tip), 0, reach - distance - 1)
    reverse_turn = jnp.where(root, 0, jnp.where(tip, 2 * n - 1, n - 1))
    mate = {"src": u * CORES + 1 - c, "dst": d}
    down = {"src": s - CORES, "dst": d}
    up = {"src": s + CORES, "dst": d}
    inward = {"src": jnp.where(u < d, s + CORES, s - CORES), "dst": d}
    side = jnp.where(u < d, 0, 1)

    def peer(j):
        return {"src": s, "dst": lax.rem(d + j, n)}

    def span(start, size):
        return pl.ds(pl.multiple_of(start, size), size)

    def remote(src, dst, send, recv, device):
        return pltpu.make_async_remote_copy(
            src_ref=src, dst_ref=dst, send_sem=send, recv_sem=recv,
            device_id=device, device_id_type=MESH,
        )

    def load(t, slot):
        return pltpu.make_async_copy(adj.at[span(t * tile, tile)], stage.at[slot], load_sem.at[slot])

    load(0, 0).start()
    if tiles > 1:
        load(1, 1).start()

    barrier = pltpu.get_barrier_semaphore()
    for j in range(1, n):
        pl.semaphore_signal(barrier, inc=1, device_id=peer(j), device_id_type=MESH)
    pl.semaphore_signal(barrier, inc=1, device_id=mate, device_id_type=MESH)

    @pl.when(u > 0)
    def _():
        pl.semaphore_signal(barrier, inc=1, device_id=down, device_id_type=MESH)

    @pl.when(u < n - 1)
    def _():
        pl.semaphore_signal(barrier, inc=1, device_id=up, device_id_type=MESH)

    xs[0, span(d * rows, rows)] = feat[...]
    pl.semaphore_wait(barrier, n + (u > 0).astype(jnp.int32) + (u < n - 1).astype(jnp.int32))

    def prepare():
        def step(t, carry):
            slot = lax.rem(t, 2)
            load(t, slot).wait()
            block = stage[slot]
            high, low = parts_of(block)
            a_hi[span(t * tile, tile)] = high
            a_lo[span(t * tile, tile)] = low
            turned_high, turned_low = parts_of(block.T)
            t_hi[t] = turned_high
            t_lo[t] = turned_low

            @pl.when(t + 2 < tiles)
            def _():
                load(t + 2, slot).start()

            return carry

        lax.fori_loop(0, tiles, step, 0)

    for l in range(layers):

        def gather(j):
            own_rows = xs.at[l, span(d * rows, rows)]
            return remote(own_rows, own_rows, gs.at[l, j], gr.at[l, n - j], peer(j))

        def gathered(i):
            rows_of = xs.at[l, span(lax.rem(d + i, n) * rows, rows)]
            return remote(rows_of, rows_of, gs.at[l, i], gr.at[l, i], peer(i))

        def place(k):
            group = lax.rem(d + lax.div(k, SPLIT), n)
            return group * rows + lax.rem(k, SPLIT) * chunk

        def spread(k, to, device):
            ref = xd.at[l, span(c * half + place(k), chunk)]
            return remote(ref, ref, zs.at[l, to, k], zr.at[l, k], device)

        def share(k):
            ref = xd.at[l, span(c * half + place(k), chunk)]
            return remote(ref, ref, cs.at[l, k], cr.at[l, k], mate)

        def spread_group(g):
            for part in range(SPLIT):
                k = g * SPLIT + part

                @pl.when(root)
                def _():
                    xd[l, span(c * half + place(k), chunk)] = xs[l, span(place(k), chunk)]

                @pl.when(jnp.logical_not(root))
                def _():
                    spread(k, 0, down).wait_recv()

                @pl.when(below)
                def _():
                    spread(k, 0, down).start()

                @pl.when(above)
                def _():
                    spread(k, 1, up).start()

                share(k).start()

        def pair(k):
            span_k = span(k * chunk, chunk)
            return remote(swap_out.at[span_k], pair_in.at[l, span_k], ps.at[l, k], pr.at[l, k], mate)

        def chain(k, which):
            span_k = span(k * chunk, chunk)
            return remote(
                own.at[span_k], chain_in.at[l, which, span_k], hs.at[l, k], hr.at[l, which, k], inward
            )

        def total(r):
            return remote(
                own.at[span(r * rows, rows)], total_in.at[l], fs.at[l, r], fr.at[l], {"src": s, "dst": r}
            )

        def reduce_group(i):
            r = lax.rem(d + 1 + i, n)
            for part in range(SPLIT):
                k = r * SPLIT + part
                span_k = span(k * chunk, chunk)
                pair(k).wait_recv()
                own[span_k] = own[span_k] + pair_in[l, span_k]

                @pl.when(below)
                def _():
                    chain(k, 0).wait_recv()
                    own[span_k] = own[span_k] + chain_in[l, 0, span_k]

                @pl.when(above)
                def _():
                    chain(k, 1).wait_recv()
                    own[span_k] = own[span_k] + chain_in[l, 1, span_k]

                @pl.when(jnp.logical_not(root))
                def _():
                    chain(k, side).start()

            @pl.when(jnp.logical_and(root, r == d))
            def _():
                total_in[l] = own[span(r * rows, rows)]

            @pl.when(jnp.logical_and(root, r != d))
            def _():
                total(r).start()

        def reverse_out(j):
            rows_of = rev.at[span(lax.rem(d + j, n) * rows, rows)]
            return remote(rows_of, rev_in.at[l, n - j], vs.at[l, j], vr.at[l, n - j], peer(j))

        def reverse():
            def arrive(k, carry):
                share(k).wait_recv()
                return carry

            lax.fori_loop(0, chunks, arrive, 0)
            rev[...] = jnp.zeros_like(rev)

            def step(t, carry):
                x_hi, x_lo = parts_of(xd[l, span(t * tile, tile)])
                rev[...] += dot3(t_hi[t], t_lo[t], x_hi, x_lo)
                return carry

            lax.fori_loop(0, tiles, step, 0)
            for j in range(1, n):
                reverse_out(j).start()

        for j in range(1, n):
            gather(j).start()
        for i in range(n):
            if i > 0:
                gathered(i).wait_recv()

            @pl.when(root)
            def _():
                spread_group(i)

            if l == 0 and i == 0:
                prepare()

        @pl.when(jnp.logical_not(root))
        def _():
            spread_group(0)

        x_hi, x_lo = parts_of(xs[l])
        xs_hi[...] = x_hi
        xs_lo[...] = x_lo
        strip = half // 2
        strip_chunks = chunks // 2

        def forward(i, carry):
            start = i * strip
            at = span((1 - c) * half + start, strip)
            swap_out[span(start, strip)] = dot3(a_hi[at], a_lo[at], xs_hi[...], xs_lo[...])

            def post(k, inner):
                pair(i * strip_chunks + k).start()
                return inner

            lax.fori_loop(0, strip_chunks, post, 0)
            return carry

        lax.fori_loop(0, 2, forward, 0)

        def forward_own(i, carry):
            start = i * strip
            at = span(c * half + start, strip)
            own[span(start, strip)] = dot3(a_hi[at], a_lo[at], xs_hi[...], xs_lo[...])
            return carry

        lax.fori_loop(0, 2, forward_own, 0)

        def turn(t, carry):
            @pl.when(t == reverse_turn)
            def _():
                reverse()

            g = jnp.where(tip, t - n, t) + 1

            @pl.when(jnp.logical_and(jnp.logical_not(root), jnp.logical_and(g >= 1, g < n)))
            def _():
                spread_group(g)

            @pl.when(jnp.logical_and(t >= lag, t < lag + n))
            def _():
                reduce_group(t - lag)

            return carry

        lax.fori_loop(0, 2 * n, turn, 0)

        back = rev[span(d * rows, rows)]
        for i in range(1, n):
            remote(
                rev.at[span(d * rows, rows)], rev_in.at[l, i], vs.at[l, i], vr.at[l, i], peer(i)
            ).wait_recv()
            back = back + rev_in[l, i]

        @pl.when(jnp.logical_not(root))
        def _():
            total(d).wait_recv()

        mixed = dot3(*parts_of(total_in[l]), *parts_of(weights[l, 0]))
        mixed = mixed + dot3(*parts_of(back), *parts_of(weights[l, 1]))
        result = jnp.maximum(mixed + biases[pl.ds(l, 1)], 0.0)
        if l + 1 < layers:
            xs[l + 1, span(d * rows, rows)] = result
        else:
            out[...] = result

        for j in range(1, n):
            gather(j).wait_send()
            reverse_out(j).wait_send()

        def drain(k, carry):
            share(k).wait_send()
            pair(k).wait_send()

            @pl.when(below)
            def _():
                spread(k, 0, down).wait_send()

            @pl.when(above)
            def _():
                spread(k, 1, up).wait_send()

            @pl.when(jnp.logical_not(root))
            def _():
                chain(k, side).wait_send()

            return carry

        lax.fori_loop(0, chunks, drain, 0)
        for r in range(n):

            @pl.when(jnp.logical_and(root, r != d))
            def _():
                total(r).wait_send()


def body(adjacency, features, layer_weights, layer_biases):
    n = lax.axis_size("dst")
    assert lax.axis_size("src") == CORES * n
    layers = layer_weights.shape[0]
    rows, width = features.shape
    half = n * rows
    tile = 256
    tiles = CORES * half // tile
    chunks = n * SPLIT
    f32, bf16 = jnp.float32, jnp.bfloat16
    dma = pltpu.SemaphoreType.DMA
    vmem = pltpu.VMEM
    scratch = [
        vmem((2, tile, half), f32),
        vmem((CORES * half, half), bf16),
        vmem((CORES * half, half), bf16),
        vmem((tiles, half, tile), bf16),
        vmem((tiles, half, tile), bf16),
        vmem((half, width), bf16),
        vmem((half, width), bf16),
        vmem((layers, half, width), f32),
        vmem((layers, CORES * half, width), f32),
        vmem((half, width), f32),
        vmem((half, width), f32),
        vmem((half, width), f32),
        vmem((layers, half, width), f32),
        vmem((layers, 2, half, width), f32),
        vmem((layers, n, rows, width), f32),
        vmem((layers, rows, width), f32),
        dma((2,)),
        dma((layers, n)),
        dma((layers, n)),
        dma((layers, 2, chunks)),
        dma((layers, chunks)),
        dma((layers, chunks)),
        dma((layers, chunks)),
        dma((layers, chunks)),
        dma((layers, chunks)),
        dma((layers, chunks)),
        dma((layers, 2, chunks)),
        dma((layers, n)),
        dma((layers,)),
        dma((layers, n)),
        dma((layers, n)),
    ]
    in_vmem = pl.BlockSpec(memory_space=pltpu.VMEM)
    flops = 2 * 3 * 2 * layers * CORES * half * half * width
    return pl.pallas_call(
        functools.partial(kernel, n, layers, tile),
        out_shape=jax.ShapeDtypeStruct((rows, width), f32),
        in_specs=[pl.BlockSpec(memory_space=pl.ANY), in_vmem, in_vmem, in_vmem],
        out_specs=in_vmem,
        scratch_shapes=scratch,
        compiler_params=pltpu.CompilerParams(
            collective_id=0, has_side_effects=True, vmem_limit_bytes=60 * 2**20
        ),
        cost_estimate=pl.CostEstimate(
            flops=flops, bytes_accessed=adjacency.size * 4, transcendentals=0
        ),
    )(adjacency, features, layer_weights, layer_biases)


def solution(mesh):
    placed = (P("dst", "src"), P(("src", "dst"), None), P(), P())
    return jax.shard_map(
        body, mesh=mesh, in_specs=placed, out_specs=P(("src", "dst"), None), check_vma=False
    )
```

```python
import functools

import jax
import jax.numpy as jnp
from jax import lax
from jax.experimental import pallas as pl
from jax.experimental.pallas import tpu as pltpu
from jax.sharding import PartitionSpec as P

MESH = pl.DeviceIdType.MESH
CORES = 2
SPLIT = 2


def parts_of(value):
    high = value.astype(jnp.bfloat16)
    return high, (value - high.astype(jnp.float32)).astype(jnp.bfloat16)


def dot3(a_high, a_low, b_high, b_low):
    dot = functools.partial(jnp.dot, preferred_element_type=jnp.float32)
    return dot(a_high, b_high) + (dot(a_high, b_low) + dot(a_low, b_high))


def kernel(
    n, layers, tile,
    adj, feat, weights, biases, out,
    stage, a_hi, a_lo, t_hi, t_lo, xs_hi, xs_lo,
    xs, xd, swap_out, own, rev, pair_in, chain_in, rev_in, total_in,
    load_sem, gs, gr, zs, zr, cs, cr, ps, pr, hs, hr, fs, fr, vs, vr,
):
    rows, width = feat.shape
    half = n * rows
    chunk = rows // SPLIT
    chunks = n * SPLIT
    tiles = CORES * half // tile
    s, d = lax.axis_index("src"), lax.axis_index("dst")
    u, c = lax.div(s, CORES), lax.rem(s, CORES)
    root = u == d
    below = jnp.logical_and(u <= d, u > 0)
    above = jnp.logical_and(u >= d, u < n - 1)
    distance = jnp.abs(u - d)
    reach = jnp.where(u < d, d, n - 1 - d)
    tip = jnp.logical_and(jnp.logical_not(root), distance == reach)
    middle = jnp.logical_not(jnp.logical_or(root, tip))
    reverse_turn = jnp.where(tip, 2 * n + 1, n)
    spread_turn = jnp.where(tip, n + 1, 0)
    reduce_turn = jnp.where(root, n, jnp.where(tip, 1, 1 + reach - distance))
    mate = {"src": u * CORES + 1 - c, "dst": d}
    down = {"src": s - CORES, "dst": d}
    up = {"src": s + CORES, "dst": d}
    inward = {"src": jnp.where(u < d, s + CORES, s - CORES), "dst": d}
    side = jnp.where(u < d, 0, 1)

    def peer(j):
        return {"src": s, "dst": lax.rem(d + j, n)}

    def span(start, size):
        return pl.ds(pl.multiple_of(start, size), size)

    def remote(src, dst, send, recv, device):
        return pltpu.make_async_remote_copy(
            src_ref=src, dst_ref=dst, send_sem=send, recv_sem=recv,
            device_id=device, device_id_type=MESH,
        )

    def load(t, slot):
        return pltpu.make_async_copy(adj.at[span(t * tile, tile)], stage.at[slot], load_sem.at[slot])

    load(0, 0).start()
    if tiles > 1:
        load(1, 1).start()

    barrier = pltpu.get_barrier_semaphore()
    for j in range(1, n):
        pl.semaphore_signal(barrier, inc=1, device_id=peer(j), device_id_type=MESH)
    pl.semaphore_signal(barrier, inc=1, device_id=mate, device_id_type=MESH)

    @pl.when(u > 0)
    def _():
        pl.semaphore_signal(barrier, inc=1, device_id=down, device_id_type=MESH)

    @pl.when(u < n - 1)
    def _():
        pl.semaphore_signal(barrier, inc=1, device_id=up, device_id_type=MESH)

    xs[0, span(d * rows, rows)] = feat[...]
    pl.semaphore_wait(barrier, n + (u > 0).astype(jnp.int32) + (u < n - 1).astype(jnp.int32))

    def prepare():
        def step(t, carry):
            slot = lax.rem(t, 2)
            load(t, slot).wait()
            block = stage[slot]
            high, low = parts_of(block)
            a_hi[span(t * tile, tile)] = high
            a_lo[span(t * tile, tile)] = low
            turned_high, turned_low = parts_of(block.T)
            t_hi[t] = turned_high
            t_lo[t] = turned_low

            @pl.when(t + 2 < tiles)
            def _():
                load(t + 2, slot).start()

            return carry

        lax.fori_loop(0, tiles, step, 0)

    for l in range(layers):

        def gather(j):
            own_rows = xs.at[l, span(d * rows, rows)]
            return remote(own_rows, own_rows, gs.at[l, j], gr.at[l, n - j], peer(j))

        def gathered(i):
            rows_of = xs.at[l, span(lax.rem(d + i, n) * rows, rows)]
            return remote(rows_of, rows_of, gs.at[l, i], gr.at[l, i], peer(i))

        def place(k):
            group = lax.rem(d + lax.div(k, SPLIT), n)
            return group * rows + lax.rem(k, SPLIT) * chunk

        def spread(k, to, device):
            ref = xd.at[l, span(c * half + place(k), chunk)]
            return remote(ref, ref, zs.at[l, to, k], zr.at[l, k], device)

        def share(k):
            ref = xd.at[l, span(c * half + place(k), chunk)]
            return remote(ref, ref, cs.at[l, k], cr.at[l, k], mate)

        def spread_group(g):
            for part in range(SPLIT):
                k = g * SPLIT + part

                @pl.when(root)
                def _():
                    xd[l, span(c * half + place(k), chunk)] = xs[l, span(place(k), chunk)]

                @pl.when(jnp.logical_not(root))
                def _():
                    spread(k, 0, down).wait_recv()

                @pl.when(below)
                def _():
                    spread(k, 0, down).start()

                @pl.when(above)
                def _():
                    spread(k, 1, up).start()

                share(k).start()

        def pair(k):
            span_k = span(k * chunk, chunk)
            return remote(swap_out.at[span_k], pair_in.at[l, span_k], ps.at[l, k], pr.at[l, k], mate)

        def chain(k, which):
            span_k = span(k * chunk, chunk)
            return remote(
                own.at[span_k], chain_in.at[l, which, span_k], hs.at[l, k], hr.at[l, which, k], inward
            )

        def total(r):
            return remote(
                own.at[span(r * rows, rows)], total_in.at[l], fs.at[l, r], fr.at[l], {"src": s, "dst": r}
            )

        def reduce_group(i):
            r = lax.rem(d + 1 + i, n)
            for part in range(SPLIT):
                k = r * SPLIT + part
                span_k = span(k * chunk, chunk)
                pair(k).wait_recv()
                own[span_k] = own[span_k] + pair_in[l, span_k]

                @pl.when(below)
                def _():
                    chain(k, 0).wait_recv()
                    own[span_k] = own[span_k] + chain_in[l, 0, span_k]

                @pl.when(above)
                def _():
                    chain(k, 1).wait_recv()
                    own[span_k] = own[span_k] + chain_in[l, 1, span_k]

                @pl.when(jnp.logical_not(root))
                def _():
                    chain(k, side).start()

            @pl.when(jnp.logical_and(root, r == d))
            def _():
                total_in[l] = own[span(r * rows, rows)]

            @pl.when(jnp.logical_and(root, r != d))
            def _():
                total(r).start()

        def reverse_out(j):
            rows_of = rev.at[span(lax.rem(d + j, n) * rows, rows)]
            return remote(rows_of, rev_in.at[l, n - j], vs.at[l, j], vr.at[l, n - j], peer(j))

        def reverse():
            def arrive(k, carry):
                share(k).wait_recv()
                return carry

            lax.fori_loop(0, chunks, arrive, 0)
            rev[...] = jnp.zeros_like(rev)

            def step(t, carry):
                x_hi, x_lo = parts_of(xd[l, span(t * tile, tile)])
                rev[...] += dot3(t_hi[t], t_lo[t], x_hi, x_lo)
                return carry

            lax.fori_loop(0, tiles, step, 0)
            for j in range(1, n):
                reverse_out(j).start()

        for j in range(1, n):
            gather(j).start()
        for i in range(n):
            if i > 0:
                gathered(i).wait_recv()

            @pl.when(root)
            def _():
                spread_group(i)

            @pl.when(jnp.logical_and(middle, distance == i))
            def _():
                spread_group(0)

            if l == 0 and i == 0:
                prepare()

        x_hi, x_lo = parts_of(xs[l])
        xs_hi[...] = x_hi
        xs_lo[...] = x_lo

        def forward(i):
            start = lax.rem(d + 1 + i, n) * rows
            at = span((1 - c) * half + start, rows)
            swap_out[span(start, rows)] = dot3(a_hi[at], a_lo[at], xs_hi[...], xs_lo[...])
            for part in range(SPLIT):
                pair(lax.rem(d + 1 + i, n) * SPLIT + part).start()
            at = span(c * half + start, rows)
            own[span(start, rows)] = dot3(a_hi[at], a_lo[at], xs_hi[...], xs_lo[...])

        def turn(t, carry):
            @pl.when(t < n)
            def _():
                forward(t)

            @pl.when(t == reverse_turn)
            def _():
                reverse()

            g = t - spread_turn
            first = jnp.where(middle, 1, 0)

            @pl.when(jnp.logical_and(jnp.logical_not(root), jnp.logical_and(g >= first, g < n)))
            def _():
                spread_group(g)

            i = t - reduce_turn

            @pl.when(jnp.logical_and(i >= 0, i < n))
            def _():
                reduce_group(i)

            return carry

        lax.fori_loop(0, 2 * n + 2, turn, 0)

        back = rev[span(d * rows, rows)]
        for i in range(1, n):
            remote(
                rev.at[span(d * rows, rows)], rev_in.at[l, i], vs.at[l, i], vr.at[l, i], peer(i)
            ).wait_recv()
            back = back + rev_in[l, i]

        @pl.when(jnp.logical_not(root))
        def _():
            total(d).wait_recv()

        mixed = dot3(*parts_of(total_in[l]), *parts_of(weights[l, 0]))
        mixed = mixed + dot3(*parts_of(back), *parts_of(weights[l, 1]))
        result = jnp.maximum(mixed + biases[pl.ds(l, 1)], 0.0)
        if l + 1 < layers:
            xs[l + 1, span(d * rows, rows)] = result
        else:
            out[...] = result

        for j in range(1, n):
            gather(j).wait_send()
            reverse_out(j).wait_send()

        def drain(k, carry):
            share(k).wait_send()
            pair(k).wait_send()

            @pl.when(below)
            def _():
                spread(k, 0, down).wait_send()

            @pl.when(above)
            def _():
                spread(k, 1, up).wait_send()

            @pl.when(jnp.logical_not(root))
            def _():
                chain(k, side).wait_send()

            return carry

        lax.fori_loop(0, chunks, drain, 0)
        for r in range(n):

            @pl.when(jnp.logical_and(root, r != d))
            def _():
                total(r).wait_send()


def body(adjacency, features, layer_weights, layer_biases):
    n = lax.axis_size("dst")
    assert lax.axis_size("src") == CORES * n
    layers = layer_weights.shape[0]
    rows, width = features.shape
    half = n * rows
    tile = 256
    tiles = CORES * half // tile
    chunks = n * SPLIT
    f32, bf16 = jnp.float32, jnp.bfloat16
    dma = pltpu.SemaphoreType.DMA
    vmem = pltpu.VMEM
    scratch = [
        vmem((2, tile, half), f32),
        vmem((CORES * half, half), bf16),
        vmem((CORES * half, half), bf16),
        vmem((tiles, half, tile), bf16),
        vmem((tiles, half, tile), bf16),
        vmem((half, width), bf16),
        vmem((half, width), bf16),
        vmem((layers, half, width), f32),
        vmem((layers, CORES * half, width), f32),
        vmem((half, width), f32),
        vmem((half, width), f32),
        vmem((half, width), f32),
        vmem((layers, half, width), f32),
        vmem((layers, 2, half, width), f32),
        vmem((layers, n, rows, width), f32),
        vmem((layers, rows, width), f32),
        dma((2,)),
        dma((layers, n)),
        dma((layers, n)),
        dma((layers, 2, chunks)),
        dma((layers, chunks)),
        dma((layers, chunks)),
        dma((layers, chunks)),
        dma((layers, chunks)),
        dma((layers, chunks)),
        dma((layers, chunks)),
        dma((layers, 2, chunks)),
        dma((layers, n)),
        dma((layers,)),
        dma((layers, n)),
        dma((layers, n)),
    ]
    in_vmem = pl.BlockSpec(memory_space=pltpu.VMEM)
    flops = 2 * 3 * 2 * layers * CORES * half * half * width
    return pl.pallas_call(
        functools.partial(kernel, n, layers, tile),
        out_shape=jax.ShapeDtypeStruct((rows, width), f32),
        in_specs=[pl.BlockSpec(memory_space=pl.ANY), in_vmem, in_vmem, in_vmem],
        out_specs=in_vmem,
        scratch_shapes=scratch,
        compiler_params=pltpu.CompilerParams(
            collective_id=0, has_side_effects=True, vmem_limit_bytes=60 * 2**20
        ),
        cost_estimate=pl.CostEstimate(
            flops=flops, bytes_accessed=adjacency.size * 4, transcendentals=0
        ),
    )(adjacency, features, layer_weights, layer_biases)


def solution(mesh):
    placed = (P("dst", "src"), P(("src", "dst"), None), P(), P())
    return jax.shard_map(
        body, mesh=mesh, in_specs=placed, out_specs=P(("src", "dst"), None), check_vma=False
    )
```

```python
import functools

import jax
import jax.numpy as jnp
from jax import lax
from jax.experimental import pallas as pl
from jax.experimental.pallas import tpu as pltpu
from jax.sharding import PartitionSpec as P

MESH = pl.DeviceIdType.MESH
CORES = 2
SPLIT = 2


def parts_of(value):
    high = value.astype(jnp.bfloat16)
    return high, (value - high.astype(jnp.float32)).astype(jnp.bfloat16)


def dot3(a_high, a_low, b_high, b_low):
    dot = functools.partial(jnp.dot, preferred_element_type=jnp.float32)
    return dot(a_high, b_high) + (dot(a_high, b_low) + dot(a_low, b_high))


def kernel(
    n, layers, tile,
    adj, feat, weights, biases, out,
    stage, a_hi, a_lo, t_hi, t_lo, xs_hi, xs_lo,
    xs, xd, swap_out, own, rev, pair_in, chain_in, rev_in, total_in,
    load_sem, gs, gr, zs, zr, cs, cr, ps, pr, hs, hr, fs, fr, vs, vr,
):
    rows, width = feat.shape
    half = n * rows
    chunk = rows // SPLIT
    chunks = n * SPLIT
    tiles = CORES * half // tile
    s, d = lax.axis_index("src"), lax.axis_index("dst")
    u, c = lax.div(s, CORES), lax.rem(s, CORES)
    root = u == d
    below = jnp.logical_and(u <= d, u > 0)
    above = jnp.logical_and(u >= d, u < n - 1)
    distance = jnp.abs(u - d)
    reach = jnp.where(u < d, d, n - 1 - d)
    tip = jnp.logical_and(jnp.logical_not(root), distance == reach)
    middle = jnp.logical_not(jnp.logical_or(root, tip))
    reverse_turn = jnp.where(tip, 2 * n + 1, n)
    spread_turn = jnp.where(tip, n + 1, 0)
    reduce_turn = jnp.where(root, n, jnp.where(tip, 1, 1 + reach - distance))
    mate = {"src": u * CORES + 1 - c, "dst": d}
    down = {"src": s - CORES, "dst": d}
    up = {"src": s + CORES, "dst": d}
    inward = {"src": jnp.where(u < d, s + CORES, s - CORES), "dst": d}
    side = jnp.where(u < d, 0, 1)

    def peer(j):
        return {"src": s, "dst": lax.rem(d + j, n)}

    def span(start, size):
        return pl.ds(pl.multiple_of(start, size), size)

    def remote(src, dst, send, recv, device):
        return pltpu.make_async_remote_copy(
            src_ref=src, dst_ref=dst, send_sem=send, recv_sem=recv,
            device_id=device, device_id_type=MESH,
        )

    def load(t, slot):
        return pltpu.make_async_copy(adj.at[span(t * tile, tile)], stage.at[slot], load_sem.at[slot])

    load(0, 0).start()
    if tiles > 1:
        load(1, 1).start()

    barrier = pltpu.get_barrier_semaphore()
    for j in range(1, n):
        pl.semaphore_signal(barrier, inc=1, device_id=peer(j), device_id_type=MESH)
    pl.semaphore_signal(barrier, inc=1, device_id=mate, device_id_type=MESH)

    @pl.when(u > 0)
    def _():
        pl.semaphore_signal(barrier, inc=1, device_id=down, device_id_type=MESH)

    @pl.when(u < n - 1)
    def _():
        pl.semaphore_signal(barrier, inc=1, device_id=up, device_id_type=MESH)

    xs[0, span(d * rows, rows)] = feat[...]
    pl.semaphore_wait(barrier, n + (u > 0).astype(jnp.int32) + (u < n - 1).astype(jnp.int32))

    def prepare():
        def step(t, carry):
            slot = lax.rem(t, 2)
            load(t, slot).wait()
            block = stage[slot]
            high, low = parts_of(block)
            a_hi[span(t * tile, tile)] = high
            a_lo[span(t * tile, tile)] = low
            turned_high, turned_low = parts_of(block.T)
            t_hi[t] = turned_high
            t_lo[t] = turned_low

            @pl.when(t + 2 < tiles)
            def _():
                load(t + 2, slot).start()

            return carry

        lax.fori_loop(0, tiles, step, 0)

    def gather(l, j):
        own_rows = xs.at[l, span(d * rows, rows)]
        return remote(own_rows, own_rows, gs.at[l, j], gr.at[l, n - j], peer(j))

    def place(k):
        group = lax.rem(d + lax.div(k, SPLIT), n)
        return group * rows + lax.rem(k, SPLIT) * chunk

    def spread(l, k, to, device):
        ref = xd.at[l, span(c * half + place(k), chunk)]
        return remote(ref, ref, zs.at[l, to, k], zr.at[l, k], device)

    def share(l, k):
        ref = xd.at[l, span(c * half + place(k), chunk)]
        return remote(ref, ref, cs.at[l, k], cr.at[l, k], mate)

    def spread_group(l, g):
        for part in range(SPLIT):
            k = g * SPLIT + part

            @pl.when(root)
            def _():
                xd[l, span(c * half + place(k), chunk)] = xs[l, span(place(k), chunk)]

            @pl.when(jnp.logical_not(root))
            def _():
                spread(l, k, 0, down).wait_recv()

            @pl.when(below)
            def _():
                spread(l, k, 0, down).start()

            @pl.when(above)
            def _():
                spread(l, k, 1, up).start()

            share(l, k).start()

    def begin(l):
        for j in range(1, n):
            gather(l, j).start()

        @pl.when(root)
        def _():
            spread_group(l, 0)

    begin(0)
    prepare()

    for l in range(layers):

        def gathered(i):
            rows_of = xs.at[l, span(lax.rem(d + i, n) * rows, rows)]
            return remote(rows_of, rows_of, gs.at[l, i], gr.at[l, i], peer(i))

        def pair(k):
            span_k = span(k * chunk, chunk)
            return remote(swap_out.at[span_k], pair_in.at[l, span_k], ps.at[l, k], pr.at[l, k], mate)

        def chain(k, which):
            span_k = span(k * chunk, chunk)
            return remote(
                own.at[span_k], chain_in.at[l, which, span_k], hs.at[l, k], hr.at[l, which, k], inward
            )

        def total(r):
            return remote(
                own.at[span(r * rows, rows)], total_in.at[l], fs.at[l, r], fr.at[l], {"src": s, "dst": r}
            )

        def reduce_group(i):
            r = lax.rem(d + 1 + i, n)
            for part in range(SPLIT):
                k = r * SPLIT + part
                span_k = span(k * chunk, chunk)
                pair(k).wait_recv()
                own[span_k] = own[span_k] + pair_in[l, span_k]

                @pl.when(below)
                def _():
                    chain(k, 0).wait_recv()
                    own[span_k] = own[span_k] + chain_in[l, 0, span_k]

                @pl.when(above)
                def _():
                    chain(k, 1).wait_recv()
                    own[span_k] = own[span_k] + chain_in[l, 1, span_k]

                @pl.when(jnp.logical_not(root))
                def _():
                    chain(k, side).start()

            @pl.when(jnp.logical_and(root, r == d))
            def _():
                total_in[l] = own[span(r * rows, rows)]

            @pl.when(jnp.logical_and(root, r != d))
            def _():
                total(r).start()

        def reverse_out(j):
            rows_of = rev.at[span(lax.rem(d + j, n) * rows, rows)]
            return remote(rows_of, rev_in.at[l, n - j], vs.at[l, j], vr.at[l, n - j], peer(j))

        def reverse():
            def arrive(k, carry):
                share(l, k).wait_recv()
                return carry

            lax.fori_loop(0, chunks, arrive, 0)
            rev[...] = jnp.zeros_like(rev)

            def step(t, carry):
                x_hi, x_lo = parts_of(xd[l, span(t * tile, tile)])
                rev[...] += dot3(t_hi[t], t_lo[t], x_hi, x_lo)
                return carry

            lax.fori_loop(0, tiles, step, 0)
            for j in range(1, n):
                reverse_out(j).start()

        for i in range(1, n):
            gathered(i).wait_recv()

            @pl.when(root)
            def _():
                spread_group(l, i)

            @pl.when(jnp.logical_and(middle, distance == i))
            def _():
                spread_group(l, 0)

        x_hi, x_lo = parts_of(xs[l])
        xs_hi[...] = x_hi
        xs_lo[...] = x_lo

        def forward(i):
            start = lax.rem(d + 1 + i, n) * rows
            at = span((1 - c) * half + start, rows)
            swap_out[span(start, rows)] = dot3(a_hi[at], a_lo[at], xs_hi[...], xs_lo[...])
            for part in range(SPLIT):
                pair(lax.rem(d + 1 + i, n) * SPLIT + part).start()
            at = span(c * half + start, rows)
            own[span(start, rows)] = dot3(a_hi[at], a_lo[at], xs_hi[...], xs_lo[...])

        def turn(t, carry):
            @pl.when(t < n)
            def _():
                forward(t)

            @pl.when(t == reverse_turn)
            def _():
                reverse()

            g = t - spread_turn
            first = jnp.where(middle, 1, 0)

            @pl.when(jnp.logical_and(jnp.logical_not(root), jnp.logical_and(g >= first, g < n)))
            def _():
                spread_group(l, g)

            i = t - reduce_turn

            @pl.when(jnp.logical_and(i >= 0, i < n))
            def _():
                reduce_group(i)

            return carry

        lax.fori_loop(0, 2 * n + 2, turn, 0)

        back = rev[span(d * rows, rows)]
        for i in range(1, n):
            remote(
                rev.at[span(d * rows, rows)], rev_in.at[l, i], vs.at[l, i], vr.at[l, i], peer(i)
            ).wait_recv()
            back = back + rev_in[l, i]

        mixed = dot3(*parts_of(back), *parts_of(weights[l, 1])) + biases[pl.ds(l, 1)]

        @pl.when(jnp.logical_not(root))
        def _():
            total(d).wait_recv()

        mixed = mixed + dot3(*parts_of(total_in[l]), *parts_of(weights[l, 0]))
        result = jnp.maximum(mixed, 0.0)
        if l + 1 < layers:
            xs[l + 1, span(d * rows, rows)] = result
            begin(l + 1)
        else:
            out[...] = result

        for j in range(1, n):
            gather(l, j).wait_send()
            reverse_out(j).wait_send()

        def drain(k, carry):
            share(l, k).wait_send()
            pair(k).wait_send()

            @pl.when(below)
            def _():
                spread(l, k, 0, down).wait_send()

            @pl.when(above)
            def _():
                spread(l, k, 1, up).wait_send()

            @pl.when(jnp.logical_not(root))
            def _():
                chain(k, side).wait_send()

            return carry

        lax.fori_loop(0, chunks, drain, 0)
        for r in range(n):

            @pl.when(jnp.logical_and(root, r != d))
            def _():
                total(r).wait_send()


def body(adjacency, features, layer_weights, layer_biases):
    n = lax.axis_size("dst")
    assert lax.axis_size("src") == CORES * n
    layers = layer_weights.shape[0]
    rows, width = features.shape
    half = n * rows
    tile = 256
    tiles = CORES * half // tile
    chunks = n * SPLIT
    f32, bf16 = jnp.float32, jnp.bfloat16
    dma = pltpu.SemaphoreType.DMA
    vmem = pltpu.VMEM
    scratch = [
        vmem((2, tile, half), f32),
        vmem((CORES * half, half), bf16),
        vmem((CORES * half, half), bf16),
        vmem((tiles, half, tile), bf16),
        vmem((tiles, half, tile), bf16),
        vmem((half, width), bf16),
        vmem((half, width), bf16),
        vmem((layers, half, width), f32),
        vmem((layers, CORES * half, width), f32),
        vmem((half, width), f32),
        vmem((half, width), f32),
        vmem((half, width), f32),
        vmem((layers, half, width), f32),
        vmem((layers, 2, half, width), f32),
        vmem((layers, n, rows, width), f32),
        vmem((layers, rows, width), f32),
        dma((2,)),
        dma((layers, n)),
        dma((layers, n)),
        dma((layers, 2, chunks)),
        dma((layers, chunks)),
        dma((layers, chunks)),
        dma((layers, chunks)),
        dma((layers, chunks)),
        dma((layers, chunks)),
        dma((layers, chunks)),
        dma((layers, 2, chunks)),
        dma((layers, n)),
        dma((layers,)),
        dma((layers, n)),
        dma((layers, n)),
    ]
    in_vmem = pl.BlockSpec(memory_space=pltpu.VMEM)
    flops = 2 * 3 * 2 * layers * CORES * half * half * width
    return pl.pallas_call(
        functools.partial(kernel, n, layers, tile),
        out_shape=jax.ShapeDtypeStruct((rows, width), f32),
        in_specs=[pl.BlockSpec(memory_space=pl.ANY), in_vmem, in_vmem, in_vmem],
        out_specs=in_vmem,
        scratch_shapes=scratch,
        compiler_params=pltpu.CompilerParams(
            collective_id=0, has_side_effects=True, vmem_limit_bytes=60 * 2**20
        ),
        cost_estimate=pl.CostEstimate(
            flops=flops, bytes_accessed=adjacency.size * 4, transcendentals=0
        ),
    )(adjacency, features, layer_weights, layer_biases)


def solution(mesh):
    placed = (P("dst", "src"), P(("src", "dst"), None), P(), P())
    return jax.shard_map(
        body, mesh=mesh, in_specs=placed, out_specs=P(("src", "dst"), None), check_vma=False
    )
```

```python
import functools

import jax
import jax.numpy as jnp
from jax import lax
from jax.experimental import pallas as pl
from jax.experimental.pallas import tpu as pltpu
from jax.sharding import PartitionSpec as P

MESH = pl.DeviceIdType.MESH
CORES = 2
SPLIT = 2


def parts_of(value):
    high = value.astype(jnp.bfloat16)
    return high, (value - high.astype(jnp.float32)).astype(jnp.bfloat16)


def dot3(a_high, a_low, b_high, b_low):
    dot = functools.partial(jnp.dot, preferred_element_type=jnp.float32)
    return dot(a_high, b_high) + (dot(a_high, b_low) + dot(a_low, b_high))


def kernel(
    n, layers, tile,
    adj, feat, weights, biases, out,
    stage, a_hi, a_lo, t_hi, t_lo, xs_hi, xs_lo, xd_hi, xd_lo,
    xs, xd, swap_out, own, rev, pair_in, chain_in, rev_in, total_in,
    load_sem, gs, gr, zs, zr, cs, cr, ps, pr, hs, hr, fs, fr, vs, vr,
):
    rows, width = feat.shape
    half = n * rows
    chunk = rows // SPLIT
    chunks = n * SPLIT
    tiles = CORES * half // tile
    s, d = lax.axis_index("src"), lax.axis_index("dst")
    u, c = lax.div(s, CORES), lax.rem(s, CORES)
    root = u == d
    below = jnp.logical_and(u <= d, u > 0)
    above = jnp.logical_and(u >= d, u < n - 1)
    distance = jnp.abs(u - d)
    reach = jnp.where(u < d, d, n - 1 - d)
    tip = jnp.logical_and(jnp.logical_not(root), distance == reach)
    middle = jnp.logical_not(jnp.logical_or(root, tip))
    reverse_turn = jnp.where(tip, 2 * n + 1, n)
    spread_turn = jnp.where(tip, n + 1, 0)
    reduce_turn = jnp.where(root, n, jnp.where(tip, 1, 1 + reach - distance))
    mate = {"src": u * CORES + 1 - c, "dst": d}
    down = {"src": s - CORES, "dst": d}
    up = {"src": s + CORES, "dst": d}
    inward = {"src": jnp.where(u < d, s + CORES, s - CORES), "dst": d}
    side = jnp.where(u < d, 0, 1)

    def peer(j):
        return {"src": s, "dst": lax.rem(d + j, n)}

    def span(start, size):
        return pl.ds(pl.multiple_of(start, size), size)

    def remote(src, dst, send, recv, device):
        return pltpu.make_async_remote_copy(
            src_ref=src, dst_ref=dst, send_sem=send, recv_sem=recv,
            device_id=device, device_id_type=MESH,
        )

    def load(t, slot):
        return pltpu.make_async_copy(adj.at[span(t * tile, tile)], stage.at[slot], load_sem.at[slot])

    load(0, 0).start()
    if tiles > 1:
        load(1, 1).start()

    barrier = pltpu.get_barrier_semaphore()
    for j in range(1, n):
        pl.semaphore_signal(barrier, inc=1, device_id=peer(j), device_id_type=MESH)
    pl.semaphore_signal(barrier, inc=1, device_id=mate, device_id_type=MESH)

    @pl.when(u > 0)
    def _():
        pl.semaphore_signal(barrier, inc=1, device_id=down, device_id_type=MESH)

    @pl.when(u < n - 1)
    def _():
        pl.semaphore_signal(barrier, inc=1, device_id=up, device_id_type=MESH)

    xs[0, span(d * rows, rows)] = feat[...]
    pl.semaphore_wait(barrier, n + (u > 0).astype(jnp.int32) + (u < n - 1).astype(jnp.int32))

    def prepare():
        def step(t, carry):
            slot = lax.rem(t, 2)
            load(t, slot).wait()
            block = stage[slot]
            high, low = parts_of(block)
            a_hi[span(t * tile, tile)] = high
            a_lo[span(t * tile, tile)] = low
            turned_high, turned_low = parts_of(block.T)
            t_hi[t] = turned_high
            t_lo[t] = turned_low

            @pl.when(t + 2 < tiles)
            def _():
                load(t + 2, slot).start()

            return carry

        lax.fori_loop(0, tiles, step, 0)

    def gather(l, j):
        own_rows = xs.at[l, span(d * rows, rows)]
        return remote(own_rows, own_rows, gs.at[l, j], gr.at[l, n - j], peer(j))

    def place(k):
        group = lax.rem(d + lax.div(k, SPLIT), n)
        return group * rows + lax.rem(k, SPLIT) * chunk

    def spread(l, k, to, device):
        ref = xd.at[l, span(c * half + place(k), chunk)]
        return remote(ref, ref, zs.at[l, to, k], zr.at[l, k], device)

    def share(l, k):
        ref = xd.at[l, span(c * half + place(k), chunk)]
        return remote(ref, ref, cs.at[l, k], cr.at[l, k], mate)

    def spread_group(l, g):
        for part in range(SPLIT):
            k = g * SPLIT + part

            @pl.when(root)
            def _():
                xd[l, span(c * half + place(k), chunk)] = xs[l, span(place(k), chunk)]

            @pl.when(jnp.logical_not(root))
            def _():
                spread(l, k, 0, down).wait_recv()

            @pl.when(below)
            def _():
                spread(l, k, 0, down).start()

            @pl.when(above)
            def _():
                spread(l, k, 1, up).start()

            share(l, k).start()

    def begin(l):
        for m in range(n):
            j = lax.rem(u + m - d + n, n)

            @pl.when(j != 0)
            def _():
                gather(l, j).start()

        @pl.when(root)
        def _():
            spread_group(l, 0)

    begin(0)
    prepare()

    for l in range(layers):

        def gathered(i):
            rows_of = xs.at[l, span(lax.rem(d + i, n) * rows, rows)]
            return remote(rows_of, rows_of, gs.at[l, i], gr.at[l, i], peer(i))

        def pair(k):
            span_k = span(k * chunk, chunk)
            return remote(swap_out.at[span_k], pair_in.at[l, span_k], ps.at[l, k], pr.at[l, k], mate)

        def chain(k, which):
            span_k = span(k * chunk, chunk)
            return remote(
                own.at[span_k], chain_in.at[l, which, span_k], hs.at[l, k], hr.at[l, which, k], inward
            )

        def total(r):
            return remote(
                own.at[span(r * rows, rows)], total_in.at[l], fs.at[l, r], fr.at[l], {"src": s, "dst": r}
            )

        def reduce_group(i):
            r = lax.rem(d + 1 + i, n)
            for part in range(SPLIT):
                k = r * SPLIT + part
                span_k = span(k * chunk, chunk)
                pair(k).wait_recv()
                own[span_k] = own[span_k] + pair_in[l, span_k]

                @pl.when(below)
                def _():
                    chain(k, 0).wait_recv()
                    own[span_k] = own[span_k] + chain_in[l, 0, span_k]

                @pl.when(above)
                def _():
                    chain(k, 1).wait_recv()
                    own[span_k] = own[span_k] + chain_in[l, 1, span_k]

                @pl.when(jnp.logical_not(root))
                def _():
                    chain(k, side).start()

            @pl.when(jnp.logical_and(root, r == d))
            def _():
                total_in[l] = own[span(r * rows, rows)]

            @pl.when(jnp.logical_and(root, r != d))
            def _():
                total(r).start()

        def reverse_out(j):
            rows_of = rev.at[span(lax.rem(d + j, n) * rows, rows)]
            return remote(rows_of, rev_in.at[l, n - j], vs.at[l, j], vr.at[l, n - j], peer(j))

        def reverse():
            def arrive(k, carry):
                share(l, k).wait_recv()
                return carry

            lax.fori_loop(0, chunks, arrive, 0)
            x_hi, x_lo = parts_of(xd[l])
            xd_hi[...] = x_hi
            xd_lo[...] = x_lo

            def group(i, carry):
                rows_of = span(lax.rem(d + 1 + i, n) * rows, rows)
                total_rows = jnp.zeros((rows, width), jnp.float32)
                for t in range(tiles):
                    at = pl.ds(t * tile, tile)
                    total_rows += dot3(t_hi[t, rows_of], t_lo[t, rows_of], xd_hi[at], xd_lo[at])
                rev[rows_of] = total_rows

                @pl.when(i < n - 1)
                def _():
                    reverse_out(i + 1).start()

                return carry

            lax.fori_loop(0, n, group, 0)

        for i in range(1, n):
            gathered(i).wait_recv()

            @pl.when(root)
            def _():
                spread_group(l, i)

            @pl.when(jnp.logical_and(middle, distance == i))
            def _():
                spread_group(l, 0)

        x_hi, x_lo = parts_of(xs[l])
        xs_hi[...] = x_hi
        xs_lo[...] = x_lo

        def forward(i):
            start = lax.rem(d + 1 + i, n) * rows
            at = span((1 - c) * half + start, rows)
            swap_out[span(start, rows)] = dot3(a_hi[at], a_lo[at], xs_hi[...], xs_lo[...])
            for part in range(SPLIT):
                pair(lax.rem(d + 1 + i, n) * SPLIT + part).start()
            at = span(c * half + start, rows)
            own[span(start, rows)] = dot3(a_hi[at], a_lo[at], xs_hi[...], xs_lo[...])

        def turn(t, carry):
            @pl.when(t < n)
            def _():
                forward(t)

            @pl.when(t == reverse_turn)
            def _():
                reverse()

            g = t - spread_turn
            first = jnp.where(middle, 1, 0)

            @pl.when(jnp.logical_and(jnp.logical_not(root), jnp.logical_and(g >= first, g < n)))
            def _():
                spread_group(l, g)

            i = t - reduce_turn

            @pl.when(jnp.logical_and(i >= 0, i < n))
            def _():
                reduce_group(i)

            return carry

        lax.fori_loop(0, 2 * n + 2, turn, 0)

        back = rev[span(d * rows, rows)]
        for i in range(1, n):
            remote(
                rev.at[span(d * rows, rows)], rev_in.at[l, i], vs.at[l, i], vr.at[l, i], peer(i)
            ).wait_recv()
            back = back + rev_in[l, i]

        mixed = dot3(*parts_of(back), *parts_of(weights[l, 1])) + biases[pl.ds(l, 1)]

        @pl.when(jnp.logical_not(root))
        def _():
            total(d).wait_recv()

        mixed = mixed + dot3(*parts_of(total_in[l]), *parts_of(weights[l, 0]))
        result = jnp.maximum(mixed, 0.0)
        if l + 1 < layers:
            xs[l + 1, span(d * rows, rows)] = result
            begin(l + 1)
        else:
            out[...] = result

        for j in range(1, n):
            gather(l, j).wait_send()
            reverse_out(j).wait_send()

        def drain(k, carry):
            share(l, k).wait_send()
            pair(k).wait_send()

            @pl.when(below)
            def _():
                spread(l, k, 0, down).wait_send()

            @pl.when(above)
            def _():
                spread(l, k, 1, up).wait_send()

            @pl.when(jnp.logical_not(root))
            def _():
                chain(k, side).wait_send()

            return carry

        lax.fori_loop(0, chunks, drain, 0)
        for r in range(n):

            @pl.when(jnp.logical_and(root, r != d))
            def _():
                total(r).wait_send()


def body(adjacency, features, layer_weights, layer_biases):
    n = lax.axis_size("dst")
    assert lax.axis_size("src") == CORES * n
    layers = layer_weights.shape[0]
    rows, width = features.shape
    half = n * rows
    tile = 256
    tiles = CORES * half // tile
    chunks = n * SPLIT
    f32, bf16 = jnp.float32, jnp.bfloat16
    dma = pltpu.SemaphoreType.DMA
    vmem = pltpu.VMEM
    scratch = [
        vmem((2, tile, half), f32),
        vmem((CORES * half, half), bf16),
        vmem((CORES * half, half), bf16),
        vmem((tiles, half, tile), bf16),
        vmem((tiles, half, tile), bf16),
        vmem((half, width), bf16),
        vmem((half, width), bf16),
        vmem((CORES * half, width), bf16),
        vmem((CORES * half, width), bf16),
        vmem((layers, half, width), f32),
        vmem((layers, CORES * half, width), f32),
        vmem((half, width), f32),
        vmem((half, width), f32),
        vmem((half, width), f32),
        vmem((layers, half, width), f32),
        vmem((layers, 2, half, width), f32),
        vmem((layers, n, rows, width), f32),
        vmem((layers, rows, width), f32),
        dma((2,)),
        dma((layers, n)),
        dma((layers, n)),
        dma((layers, 2, chunks)),
        dma((layers, chunks)),
        dma((layers, chunks)),
        dma((layers, chunks)),
        dma((layers, chunks)),
        dma((layers, chunks)),
        dma((layers, chunks)),
        dma((layers, 2, chunks)),
        dma((layers, n)),
        dma((layers,)),
        dma((layers, n)),
        dma((layers, n)),
    ]
    in_vmem = pl.BlockSpec(memory_space=pltpu.VMEM)
    flops = 2 * 3 * 2 * layers * CORES * half * half * width
    return pl.pallas_call(
        functools.partial(kernel, n, layers, tile),
        out_shape=jax.ShapeDtypeStruct((rows, width), f32),
        in_specs=[pl.BlockSpec(memory_space=pl.ANY), in_vmem, in_vmem, in_vmem],
        out_specs=in_vmem,
        scratch_shapes=scratch,
        compiler_params=pltpu.CompilerParams(
            collective_id=0, has_side_effects=True, vmem_limit_bytes=60 * 2**20
        ),
        cost_estimate=pl.CostEstimate(
            flops=flops, bytes_accessed=adjacency.size * 4, transcendentals=0
        ),
    )(adjacency, features, layer_weights, layer_biases)


def solution(mesh):
    placed = (P("dst", "src"), P(("src", "dst"), None), P(), P())
    return jax.shard_map(
        body, mesh=mesh, in_specs=placed, out_specs=P(("src", "dst"), None), check_vma=False
    )
```

```python
import functools

import jax
import jax.numpy as jnp
from jax import lax
from jax.experimental import pallas as pl
from jax.experimental.pallas import tpu as pltpu
from jax.sharding import PartitionSpec as P

MESH = pl.DeviceIdType.MESH
CORES = 2
SPLIT = 4


def parts_of(value):
    high = value.astype(jnp.bfloat16)
    return high, (value - high.astype(jnp.float32)).astype(jnp.bfloat16)


def dot3(a_high, a_low, b_high, b_low):
    dot = functools.partial(jnp.dot, preferred_element_type=jnp.float32)
    return dot(a_high, b_high) + (dot(a_high, b_low) + dot(a_low, b_high))


def kernel(
    n, layers, tile,
    adj, feat, weights, biases, out,
    stage, a_hi, a_lo, t_hi, t_lo, xs_hi, xs_lo, xd_hi, xd_lo,
    xs, xd, swap_out, own, rev, pair_in, chain_in, rev_in, total_in,
    load_sem, gs, gr, zs, zr, cs, cr, ps, pr, hs, hr, fs, fr, vs, vr,
):
    rows, width = feat.shape
    half = n * rows
    chunk = rows // SPLIT
    chunks = n * SPLIT
    tiles = CORES * half // tile
    s, d = lax.axis_index("src"), lax.axis_index("dst")
    u, c = lax.div(s, CORES), lax.rem(s, CORES)
    root = u == d
    below = jnp.logical_and(u <= d, u > 0)
    above = jnp.logical_and(u >= d, u < n - 1)
    distance = jnp.abs(u - d)
    reach = jnp.where(u < d, d, n - 1 - d)
    tip = jnp.logical_and(jnp.logical_not(root), distance == reach)
    middle = jnp.logical_not(jnp.logical_or(root, tip))
    reverse_turn = jnp.where(tip, 2 * n + 1, n)
    spread_turn = jnp.where(tip, n + 1, 0)
    reduce_turn = jnp.where(root, n, jnp.where(tip, 1, 1 + reach - distance))
    mate = {"src": u * CORES + 1 - c, "dst": d}
    down = {"src": s - CORES, "dst": d}
    up = {"src": s + CORES, "dst": d}
    inward = {"src": jnp.where(u < d, s + CORES, s - CORES), "dst": d}
    side = jnp.where(u < d, 0, 1)

    def peer(j):
        return {"src": s, "dst": lax.rem(d + j, n)}

    def span(start, size):
        return pl.ds(pl.multiple_of(start, size), size)

    def remote(src, dst, send, recv, device):
        return pltpu.make_async_remote_copy(
            src_ref=src, dst_ref=dst, send_sem=send, recv_sem=recv,
            device_id=device, device_id_type=MESH,
        )

    def load(t, slot):
        return pltpu.make_async_copy(adj.at[span(t * tile, tile)], stage.at[slot], load_sem.at[slot])

    load(0, 0).start()
    if tiles > 1:
        load(1, 1).start()

    barrier = pltpu.get_barrier_semaphore()
    for j in range(1, n):
        pl.semaphore_signal(barrier, inc=1, device_id=peer(j), device_id_type=MESH)
    pl.semaphore_signal(barrier, inc=1, device_id=mate, device_id_type=MESH)

    @pl.when(u > 0)
    def _():
        pl.semaphore_signal(barrier, inc=1, device_id=down, device_id_type=MESH)

    @pl.when(u < n - 1)
    def _():
        pl.semaphore_signal(barrier, inc=1, device_id=up, device_id_type=MESH)

    xs[0, span(d * rows, rows)] = feat[...]
    pl.semaphore_wait(barrier, n + (u > 0).astype(jnp.int32) + (u < n - 1).astype(jnp.int32))

    def prepare():
        def step(t, carry):
            slot = lax.rem(t, 2)
            load(t, slot).wait()
            block = stage[slot]
            high, low = parts_of(block)
            a_hi[span(t * tile, tile)] = high
            a_lo[span(t * tile, tile)] = low
            turned_high, turned_low = parts_of(block.T)
            t_hi[t] = turned_high
            t_lo[t] = turned_low

            @pl.when(t + 2 < tiles)
            def _():
                load(t + 2, slot).start()

            return carry

        lax.fori_loop(0, tiles, step, 0)

    def gather(l, j):
        own_rows = xs.at[l, span(d * rows, rows)]
        return remote(own_rows, own_rows, gs.at[l, j], gr.at[l, n - j], peer(j))

    def place(k):
        group = lax.rem(d + lax.div(k, SPLIT), n)
        return group * rows + lax.rem(k, SPLIT) * chunk

    def spread(l, k, to, device):
        ref = xd.at[l, span(c * half + place(k), chunk)]
        return remote(ref, ref, zs.at[l, to, k], zr.at[l, k], device)

    def share(l, k):
        ref = xd.at[l, span(c * half + place(k), chunk)]
        return remote(ref, ref, cs.at[l, k], cr.at[l, k], mate)

    def spread_group(l, g):
        for part in range(SPLIT):
            k = g * SPLIT + part

            @pl.when(root)
            def _():
                xd[l, span(c * half + place(k), chunk)] = xs[l, span(place(k), chunk)]

            @pl.when(jnp.logical_not(root))
            def _():
                spread(l, k, 0, down).wait_recv()

            @pl.when(below)
            def _():
                spread(l, k, 0, down).start()

            @pl.when(above)
            def _():
                spread(l, k, 1, up).start()

            share(l, k).start()

    def begin(l):
        for m in range(n):
            j = lax.rem(u + m - d + n, n)

            @pl.when(j != 0)
            def _():
                gather(l, j).start()

        @pl.when(root)
        def _():
            spread_group(l, 0)

    begin(0)
    prepare()

    for l in range(layers):

        def gathered(i):
            rows_of = xs.at[l, span(lax.rem(d + i, n) * rows, rows)]
            return remote(rows_of, rows_of, gs.at[l, i], gr.at[l, i], peer(i))

        def pair(k):
            span_k = span(k * chunk, chunk)
            return remote(swap_out.at[span_k], pair_in.at[l, span_k], ps.at[l, k], pr.at[l, k], mate)

        def chain(k, which):
            span_k = span(k * chunk, chunk)
            return remote(
                own.at[span_k], chain_in.at[l, which, span_k], hs.at[l, k], hr.at[l, which, k], inward
            )

        def total(r):
            return remote(
                own.at[span(r * rows, rows)], total_in.at[l], fs.at[l, r], fr.at[l], {"src": s, "dst": r}
            )

        def reduce_group(i):
            r = lax.rem(d + 1 + i, n)
            for part in range(SPLIT):
                k = r * SPLIT + part
                span_k = span(k * chunk, chunk)
                pair(k).wait_recv()
                own[span_k] = own[span_k] + pair_in[l, span_k]

                @pl.when(below)
                def _():
                    chain(k, 0).wait_recv()
                    own[span_k] = own[span_k] + chain_in[l, 0, span_k]

                @pl.when(above)
                def _():
                    chain(k, 1).wait_recv()
                    own[span_k] = own[span_k] + chain_in[l, 1, span_k]

                @pl.when(jnp.logical_not(root))
                def _():
                    chain(k, side).start()

            @pl.when(jnp.logical_and(root, r == d))
            def _():
                total_in[l] = own[span(r * rows, rows)]

            @pl.when(jnp.logical_and(root, r != d))
            def _():
                total(r).start()

        def reverse_out(j):
            rows_of = rev.at[span(lax.rem(d + j, n) * rows, rows)]
            return remote(rows_of, rev_in.at[l, n - j], vs.at[l, j], vr.at[l, n - j], peer(j))

        def reverse():
            def arrive(k, carry):
                share(l, k).wait_recv()
                return carry

            lax.fori_loop(0, chunks, arrive, 0)
            x_hi, x_lo = parts_of(xd[l])
            xd_hi[...] = x_hi
            xd_lo[...] = x_lo

            def group(i, carry):
                rows_of = span(lax.rem(d + 1 + i, n) * rows, rows)
                total_rows = jnp.zeros((rows, width), jnp.float32)
                for t in range(tiles):
                    at = pl.ds(t * tile, tile)
                    total_rows += dot3(t_hi[t, rows_of], t_lo[t, rows_of], xd_hi[at], xd_lo[at])
                rev[rows_of] = total_rows

                @pl.when(i < n - 1)
                def _():
                    reverse_out(i + 1).start()

                return carry

            lax.fori_loop(0, n, group, 0)

        for i in range(1, n):
            gathered(i).wait_recv()

            @pl.when(root)
            def _():
                spread_group(l, i)

            @pl.when(jnp.logical_and(middle, distance == i))
            def _():
                spread_group(l, 0)

        x_hi, x_lo = parts_of(xs[l])
        xs_hi[...] = x_hi
        xs_lo[...] = x_lo

        def forward(i):
            start = lax.rem(d + 1 + i, n) * rows
            at = span((1 - c) * half + start, rows)
            swap_out[span(start, rows)] = dot3(a_hi[at], a_lo[at], xs_hi[...], xs_lo[...])
            for part in range(SPLIT):
                pair(lax.rem(d + 1 + i, n) * SPLIT + part).start()
            at = span(c * half + start, rows)
            own[span(start, rows)] = dot3(a_hi[at], a_lo[at], xs_hi[...], xs_lo[...])

        def turn(t, carry):
            @pl.when(t < n)
            def _():
                forward(t)

            @pl.when(t == reverse_turn)
            def _():
                reverse()

            g = t - spread_turn
            first = jnp.where(middle, 1, 0)

            @pl.when(jnp.logical_and(jnp.logical_not(root), jnp.logical_and(g >= first, g < n)))
            def _():
                spread_group(l, g)

            i = t - reduce_turn

            @pl.when(jnp.logical_and(i >= 0, i < n))
            def _():
                reduce_group(i)

            return carry

        lax.fori_loop(0, 2 * n + 2, turn, 0)

        back = rev[span(d * rows, rows)]
        for i in range(1, n):
            remote(
                rev.at[span(d * rows, rows)], rev_in.at[l, i], vs.at[l, i], vr.at[l, i], peer(i)
            ).wait_recv()
            back = back + rev_in[l, i]

        mixed = dot3(*parts_of(back), *parts_of(weights[l, 1])) + biases[pl.ds(l, 1)]

        @pl.when(jnp.logical_not(root))
        def _():
            total(d).wait_recv()

        mixed = mixed + dot3(*parts_of(total_in[l]), *parts_of(weights[l, 0]))
        result = jnp.maximum(mixed, 0.0)
        if l + 1 < layers:
            xs[l + 1, span(d * rows, rows)] = result
            begin(l + 1)
        else:
            out[...] = result

        for j in range(1, n):
            gather(l, j).wait_send()
            reverse_out(j).wait_send()

        def drain(k, carry):
            share(l, k).wait_send()
            pair(k).wait_send()

            @pl.when(below)
            def _():
                spread(l, k, 0, down).wait_send()

            @pl.when(above)
            def _():
                spread(l, k, 1, up).wait_send()

            @pl.when(jnp.logical_not(root))
            def _():
                chain(k, side).wait_send()

            return carry

        lax.fori_loop(0, chunks, drain, 0)
        for r in range(n):

            @pl.when(jnp.logical_and(root, r != d))
            def _():
                total(r).wait_send()


def body(adjacency, features, layer_weights, layer_biases):
    n = lax.axis_size("dst")
    assert lax.axis_size("src") == CORES * n
    layers = layer_weights.shape[0]
    rows, width = features.shape
    half = n * rows
    tile = 256
    tiles = CORES * half // tile
    chunks = n * SPLIT
    f32, bf16 = jnp.float32, jnp.bfloat16
    dma = pltpu.SemaphoreType.DMA
    vmem = pltpu.VMEM
    scratch = [
        vmem((2, tile, half), f32),
        vmem((CORES * half, half), bf16),
        vmem((CORES * half, half), bf16),
        vmem((tiles, half, tile), bf16),
        vmem((tiles, half, tile), bf16),
        vmem((half, width), bf16),
        vmem((half, width), bf16),
        vmem((CORES * half, width), bf16),
        vmem((CORES * half, width), bf16),
        vmem((layers, half, width), f32),
        vmem((layers, CORES * half, width), f32),
        vmem((half, width), f32),
        vmem((half, width), f32),
        vmem((half, width), f32),
        vmem((layers, half, width), f32),
        vmem((layers, 2, half, width), f32),
        vmem((layers, n, rows, width), f32),
        vmem((layers, rows, width), f32),
        dma((2,)),
        dma((layers, n)),
        dma((layers, n)),
        dma((layers, 2, chunks)),
        dma((layers, chunks)),
        dma((layers, chunks)),
        dma((layers, chunks)),
        dma((layers, chunks)),
        dma((layers, chunks)),
        dma((layers, chunks)),
        dma((layers, 2, chunks)),
        dma((layers, n)),
        dma((layers,)),
        dma((layers, n)),
        dma((layers, n)),
    ]
    in_vmem = pl.BlockSpec(memory_space=pltpu.VMEM)
    flops = 2 * 3 * 2 * layers * CORES * half * half * width
    return pl.pallas_call(
        functools.partial(kernel, n, layers, tile),
        out_shape=jax.ShapeDtypeStruct((rows, width), f32),
        in_specs=[pl.BlockSpec(memory_space=pl.ANY), in_vmem, in_vmem, in_vmem],
        out_specs=in_vmem,
        scratch_shapes=scratch,
        compiler_params=pltpu.CompilerParams(
            collective_id=0, has_side_effects=True, vmem_limit_bytes=60 * 2**20
        ),
        cost_estimate=pl.CostEstimate(
            flops=flops, bytes_accessed=adjacency.size * 4, transcendentals=0
        ),
    )(adjacency, features, layer_weights, layer_biases)


def solution(mesh):
    placed = (P("dst", "src"), P(("src", "dst"), None), P(), P())
    return jax.shard_map(
        body, mesh=mesh, in_specs=placed, out_specs=P(("src", "dst"), None), check_vma=False
    )
```

```python
import functools

import jax
import jax.numpy as jnp
from jax import lax
from jax.experimental import pallas as pl
from jax.experimental.pallas import tpu as pltpu
from jax.sharding import PartitionSpec as P

MESH = pl.DeviceIdType.MESH
CORES = 2
SPLIT = 2


def parts_of(value):
    high = value.astype(jnp.bfloat16)
    return high, (value - high.astype(jnp.float32)).astype(jnp.bfloat16)


def dot3(a_high, a_low, b_high, b_low):
    dot = functools.partial(jnp.dot, preferred_element_type=jnp.float32)
    return dot(a_high, b_high) + (dot(a_high, b_low) + dot(a_low, b_high))


def kernel(
    n, layers, tile,
    adj, feat, weights, biases, out,
    stage, a_hi, a_lo, t_hi, t_lo, xs_hi, xs_lo, xd_hi, xd_lo,
    xs, xd, swap_out, own, rev, pair_in, chain_in, rev_in, total_in,
    load_sem, gs, gr, zs, zr, cs, cr, ps, pr, hs, hr, fs, fr, vs, vr,
):
    rows, width = feat.shape
    half = n * rows
    chunk = rows // SPLIT
    chunks = n * SPLIT
    tiles = CORES * half // tile
    s, d = lax.axis_index("src"), lax.axis_index("dst")
    u, c = lax.div(s, CORES), lax.rem(s, CORES)
    root = u == d
    below = jnp.logical_and(u <= d, u > 0)
    above = jnp.logical_and(u >= d, u < n - 1)
    distance = jnp.abs(u - d)
    reach = jnp.where(u < d, d, n - 1 - d)
    tip = jnp.logical_and(jnp.logical_not(root), distance == reach)
    middle = jnp.logical_not(jnp.logical_or(root, tip))
    reverse_turn = jnp.where(tip, 2 * n + 1, n)
    spread_turn = jnp.where(tip, n + 1, 0)
    reduce_turn = jnp.where(root, 2 * n - 1, jnp.where(tip, 1, 1 + reach - distance))
    mate = {"src": u * CORES + 1 - c, "dst": d}
    down = {"src": s - CORES, "dst": d}
    up = {"src": s + CORES, "dst": d}
    inward = {"src": jnp.where(u < d, s + CORES, s - CORES), "dst": d}
    side = jnp.where(u < d, 0, 1)

    def offset(i):
        return lax.rem(jnp.where(d < n // 2, i, n - i), n)

    def group_at(i):
        return lax.rem(d + offset(i), n)

    def peer(j):
        return {"src": s, "dst": lax.rem(d + j, n)}

    def span(start, size):
        return pl.ds(pl.multiple_of(start, size), size)

    def remote(src, dst, send, recv, device):
        return pltpu.make_async_remote_copy(
            src_ref=src, dst_ref=dst, send_sem=send, recv_sem=recv,
            device_id=device, device_id_type=MESH,
        )

    def load(t, slot):
        return pltpu.make_async_copy(adj.at[span(t * tile, tile)], stage.at[slot], load_sem.at[slot])

    load(0, 0).start()
    if tiles > 1:
        load(1, 1).start()

    barrier = pltpu.get_barrier_semaphore()
    for j in range(1, n):
        pl.semaphore_signal(barrier, inc=1, device_id=peer(j), device_id_type=MESH)
    pl.semaphore_signal(barrier, inc=1, device_id=mate, device_id_type=MESH)

    @pl.when(u > 0)
    def _():
        pl.semaphore_signal(barrier, inc=1, device_id=down, device_id_type=MESH)

    @pl.when(u < n - 1)
    def _():
        pl.semaphore_signal(barrier, inc=1, device_id=up, device_id_type=MESH)

    xs[0, span(d * rows, rows)] = feat[...]
    pl.semaphore_wait(barrier, n + (u > 0).astype(jnp.int32) + (u < n - 1).astype(jnp.int32))

    def prepare():
        def step(t, carry):
            slot = lax.rem(t, 2)
            load(t, slot).wait()
            block = stage[slot]
            high, low = parts_of(block)
            a_hi[span(t * tile, tile)] = high
            a_lo[span(t * tile, tile)] = low
            turned_high, turned_low = parts_of(block.T)
            t_hi[t] = turned_high
            t_lo[t] = turned_low

            @pl.when(t + 2 < tiles)
            def _():
                load(t + 2, slot).start()

            return carry

        lax.fori_loop(0, tiles, step, 0)

    def gather(l, j):
        own_rows = xs.at[l, span(d * rows, rows)]
        return remote(own_rows, own_rows, gs.at[l, j], gr.at[l, n - j], peer(j))

    def place(k):
        return group_at(lax.div(k, SPLIT)) * rows + lax.rem(k, SPLIT) * chunk

    def spread(l, k, to, device):
        ref = xd.at[l, span(c * half + place(k), chunk)]
        return remote(ref, ref, zs.at[l, to, k], zr.at[l, k], device)

    def share(l, k):
        ref = xd.at[l, span(c * half + place(k), chunk)]
        return remote(ref, ref, cs.at[l, k], cr.at[l, k], mate)

    def spread_group(l, g):
        for part in range(SPLIT):
            k = g * SPLIT + part

            @pl.when(root)
            def _():
                xd[l, span(c * half + place(k), chunk)] = xs[l, span(place(k), chunk)]

            @pl.when(jnp.logical_not(root))
            def _():
                spread(l, k, 0, down).wait_recv()

            @pl.when(below)
            def _():
                spread(l, k, 0, down).start()

            @pl.when(above)
            def _():
                spread(l, k, 1, up).start()

            share(l, k).start()

    def begin(l):
        for m in range(n):
            j = lax.rem(u + m - d + n, n)

            @pl.when(j != 0)
            def _():
                gather(l, j).start()

        @pl.when(root)
        def _():
            spread_group(l, 0)

    begin(0)
    prepare()

    for l in range(layers):

        def gathered(i):
            rows_of = xs.at[l, span(lax.rem(d + i, n) * rows, rows)]
            return remote(rows_of, rows_of, gs.at[l, i], gr.at[l, i], peer(i))

        def pair(k):
            span_k = span(k * chunk, chunk)
            return remote(swap_out.at[span_k], pair_in.at[l, span_k], ps.at[l, k], pr.at[l, k], mate)

        def chain(k, which):
            span_k = span(k * chunk, chunk)
            return remote(
                own.at[span_k], chain_in.at[l, which, span_k], hs.at[l, k], hr.at[l, which, k], inward
            )

        def total(r):
            return remote(
                own.at[span(r * rows, rows)], total_in.at[l], fs.at[l, r], fr.at[l], {"src": s, "dst": r}
            )

        def reduce_group(i):
            r = group_at(n - 1 - i)
            for part in range(SPLIT):
                k = r * SPLIT + part
                span_k = span(k * chunk, chunk)
                pair(k).wait_recv()
                own[span_k] = own[span_k] + pair_in[l, span_k]

                @pl.when(below)
                def _():
                    chain(k, 0).wait_recv()
                    own[span_k] = own[span_k] + chain_in[l, 0, span_k]

                @pl.when(above)
                def _():
                    chain(k, 1).wait_recv()
                    own[span_k] = own[span_k] + chain_in[l, 1, span_k]

                @pl.when(jnp.logical_not(root))
                def _():
                    chain(k, side).start()

            @pl.when(jnp.logical_and(root, r == d))
            def _():
                total_in[l] = own[span(r * rows, rows)]

            @pl.when(jnp.logical_and(root, r != d))
            def _():
                total(r).start()

        def reverse_out(j):
            rows_of = rev.at[span(lax.rem(d + j, n) * rows, rows)]
            return remote(rows_of, rev_in.at[l, n - j], vs.at[l, j], vr.at[l, n - j], peer(j))

        def reverse():
            def arrive(k, carry):
                share(l, k).wait_recv()
                return carry

            lax.fori_loop(0, chunks, arrive, 0)
            x_hi, x_lo = parts_of(xd[l])
            xd_hi[...] = x_hi
            xd_lo[...] = x_lo

        def reverse_group(i):
            rows_of = span(group_at(n - 1 - i) * rows, rows)
            total_rows = jnp.zeros((rows, width), jnp.float32)
            for t in range(tiles):
                at = pl.ds(t * tile, tile)
                total_rows += dot3(t_hi[t, rows_of], t_lo[t, rows_of], xd_hi[at], xd_lo[at])
            rev[rows_of] = total_rows

            @pl.when(i < n - 1)
            def _():
                reverse_out(offset(n - 1 - i)).start()

        for i in range(1, n):
            gathered(offset(i)).wait_recv()

            @pl.when(root)
            def _():
                spread_group(l, i)

            @pl.when(jnp.logical_and(middle, distance == i))
            def _():
                spread_group(l, 0)

        x_hi, x_lo = parts_of(xs[l])
        xs_hi[...] = x_hi
        xs_lo[...] = x_lo

        def forward(i):
            r = group_at(n - 1 - i)
            start = r * rows
            at = span((1 - c) * half + start, rows)
            swap_out[span(start, rows)] = dot3(a_hi[at], a_lo[at], xs_hi[...], xs_lo[...])
            for part in range(SPLIT):
                pair(r * SPLIT + part).start()
            at = span(c * half + start, rows)
            own[span(start, rows)] = dot3(a_hi[at], a_lo[at], xs_hi[...], xs_lo[...])

        def turn(t, carry):
            @pl.when(t < n)
            def _():
                forward(t)

            @pl.when(t == reverse_turn)
            def _():
                reverse()

            q = t - reverse_turn

            @pl.when(jnp.logical_and(q >= 0, q < n))
            def _():
                reverse_group(q)

            g = t - spread_turn
            first = jnp.where(middle, 1, 0)

            @pl.when(jnp.logical_and(jnp.logical_not(root), jnp.logical_and(g >= first, g < n)))
            def _():
                spread_group(l, g)

            i = t - reduce_turn

            @pl.when(jnp.logical_and(i >= 0, i < n))
            def _():
                reduce_group(i)

            return carry

        lax.fori_loop(0, 3 * n + 1, turn, 0)

        back = rev[span(d * rows, rows)]
        for i in range(1, n):
            remote(
                rev.at[span(d * rows, rows)], rev_in.at[l, i], vs.at[l, i], vr.at[l, i], peer(i)
            ).wait_recv()
            back = back + rev_in[l, i]

        mixed = dot3(*parts_of(back), *parts_of(weights[l, 1])) + biases[pl.ds(l, 1)]

        @pl.when(jnp.logical_not(root))
        def _():
            total(d).wait_recv()

        mixed = mixed + dot3(*parts_of(total_in[l]), *parts_of(weights[l, 0]))
        result = jnp.maximum(mixed, 0.0)
        if l + 1 < layers:
            xs[l + 1, span(d * rows, rows)] = result
            begin(l + 1)
        else:
            out[...] = result

        for j in range(1, n):
            gather(l, j).wait_send()
            reverse_out(j).wait_send()

        def drain(k, carry):
            share(l, k).wait_send()
            pair(k).wait_send()

            @pl.when(below)
            def _():
                spread(l, k, 0, down).wait_send()

            @pl.when(above)
            def _():
                spread(l, k, 1, up).wait_send()

            @pl.when(jnp.logical_not(root))
            def _():
                chain(k, side).wait_send()

            return carry

        lax.fori_loop(0, chunks, drain, 0)
        for r in range(n):

            @pl.when(jnp.logical_and(root, r != d))
            def _():
                total(r).wait_send()


def body(adjacency, features, layer_weights, layer_biases):
    n = lax.axis_size("dst")
    assert lax.axis_size("src") == CORES * n
    layers = layer_weights.shape[0]
    rows, width = features.shape
    half = n * rows
    tile = 256
    tiles = CORES * half // tile
    chunks = n * SPLIT
    f32, bf16 = jnp.float32, jnp.bfloat16
    dma = pltpu.SemaphoreType.DMA
    vmem = pltpu.VMEM
    scratch = [
        vmem((2, tile, half), f32),
        vmem((CORES * half, half), bf16),
        vmem((CORES * half, half), bf16),
        vmem((tiles, half, tile), bf16),
        vmem((tiles, half, tile), bf16),
        vmem((half, width), bf16),
        vmem((half, width), bf16),
        vmem((CORES * half, width), bf16),
        vmem((CORES * half, width), bf16),
        vmem((layers, half, width), f32),
        vmem((layers, CORES * half, width), f32),
        vmem((half, width), f32),
        vmem((half, width), f32),
        vmem((half, width), f32),
        vmem((layers, half, width), f32),
        vmem((layers, 2, half, width), f32),
        vmem((layers, n, rows, width), f32),
        vmem((layers, rows, width), f32),
        dma((2,)),
        dma((layers, n)),
        dma((layers, n)),
        dma((layers, 2, chunks)),
        dma((layers, chunks)),
        dma((layers, chunks)),
        dma((layers, chunks)),
        dma((layers, chunks)),
        dma((layers, chunks)),
        dma((layers, chunks)),
        dma((layers, 2, chunks)),
        dma((layers, n)),
        dma((layers,)),
        dma((layers, n)),
        dma((layers, n)),
    ]
    in_vmem = pl.BlockSpec(memory_space=pltpu.VMEM)
    flops = 2 * 3 * 2 * layers * CORES * half * half * width
    return pl.pallas_call(
        functools.partial(kernel, n, layers, tile),
        out_shape=jax.ShapeDtypeStruct((rows, width), f32),
        in_specs=[pl.BlockSpec(memory_space=pl.ANY), in_vmem, in_vmem, in_vmem],
        out_specs=in_vmem,
        scratch_shapes=scratch,
        compiler_params=pltpu.CompilerParams(
            collective_id=0, has_side_effects=True, vmem_limit_bytes=60 * 2**20
        ),
        cost_estimate=pl.CostEstimate(
            flops=flops, bytes_accessed=adjacency.size * 4, transcendentals=0
        ),
    )(adjacency, features, layer_weights, layer_biases)


def solution(mesh):
    placed = (P("dst", "src"), P(("src", "dst"), None), P(), P())
    return jax.shard_map(
        body, mesh=mesh, in_specs=placed, out_specs=P(("src", "dst"), None), check_vma=False
    )
```

```python
import functools

import jax
import jax.numpy as jnp
from jax import lax
from jax.experimental import pallas as pl
from jax.experimental.pallas import tpu as pltpu
from jax.sharding import PartitionSpec as P

MESH = pl.DeviceIdType.MESH
CORES = 2
SPLIT = 2


def parts_of(value):
    high = value.astype(jnp.bfloat16)
    return high, (value - high.astype(jnp.float32)).astype(jnp.bfloat16)


def dot3(a_high, a_low, b_high, b_low):
    dot = functools.partial(jnp.dot, preferred_element_type=jnp.float32)
    return dot(a_high, b_high) + (dot(a_high, b_low) + dot(a_low, b_high))


def kernel(
    n, layers, tile,
    adj, feat, weights, biases, out,
    stage, a_hi, a_lo, t_hi, t_lo, xs_hi, xs_lo, xd_hi, xd_lo,
    xs, xd, swap_out, own, rev, pair_in, chain_in, rev_in, total_in,
    load_sem, gs, gr, zs, zr, cs, cr, ps, pr, hs, hr, fs, fr, vs, vr,
):
    rows, width = feat.shape
    half = n * rows
    chunk = rows // SPLIT
    chunks = n * SPLIT
    tiles = CORES * half // tile
    s, d = lax.axis_index("src"), lax.axis_index("dst")
    u, c = lax.div(s, CORES), lax.rem(s, CORES)
    root = u == d
    below = jnp.logical_and(u <= d, u > 0)
    above = jnp.logical_and(u >= d, u < n - 1)
    distance = jnp.abs(u - d)
    reach = jnp.where(u < d, d, n - 1 - d)
    tip = jnp.logical_and(jnp.logical_not(root), distance == reach)
    middle = jnp.logical_not(jnp.logical_or(root, tip))
    reverse_turn = jnp.where(tip, 2 * n + 1, n)
    spread_turn = jnp.where(tip, n + 1, 0)
    reduce_turn = jnp.where(root, 2 * n - 1, jnp.where(tip, 1, 1 + reach - distance))
    mate = {"src": u * CORES + 1 - c, "dst": d}
    down = {"src": s - CORES, "dst": d}
    up = {"src": s + CORES, "dst": d}
    inward = {"src": jnp.where(u < d, s + CORES, s - CORES), "dst": d}
    side = jnp.where(u < d, 0, 1)

    def offset(i):
        return lax.rem(jnp.where(d < n // 2, i, n - i), n)

    def group_at(i):
        return lax.rem(d + offset(i), n)

    def peer(j):
        return {"src": s, "dst": lax.rem(d + j, n)}

    def span(start, size):
        return pl.ds(pl.multiple_of(start, size), size)

    def remote(src, dst, send, recv, device):
        return pltpu.make_async_remote_copy(
            src_ref=src, dst_ref=dst, send_sem=send, recv_sem=recv,
            device_id=device, device_id_type=MESH,
        )

    def load(t, slot):
        return pltpu.make_async_copy(adj.at[span(t * tile, tile)], stage.at[slot], load_sem.at[slot])

    load(0, 0).start()
    if tiles > 1:
        load(1, 1).start()

    barrier = pltpu.get_barrier_semaphore()
    for j in range(1, n):
        pl.semaphore_signal(barrier, inc=1, device_id=peer(j), device_id_type=MESH)
    pl.semaphore_signal(barrier, inc=1, device_id=mate, device_id_type=MESH)

    @pl.when(u > 0)
    def _():
        pl.semaphore_signal(barrier, inc=1, device_id=down, device_id_type=MESH)

    @pl.when(u < n - 1)
    def _():
        pl.semaphore_signal(barrier, inc=1, device_id=up, device_id_type=MESH)

    xs[0, span(d * rows, rows)] = feat[...]
    pl.semaphore_wait(barrier, n + (u > 0).astype(jnp.int32) + (u < n - 1).astype(jnp.int32))

    def prepare():
        def step(t, carry):
            slot = lax.rem(t, 2)
            load(t, slot).wait()
            block = stage[slot]
            high, low = parts_of(block)
            a_hi[span(t * tile, tile)] = high
            a_lo[span(t * tile, tile)] = low

            @pl.when(t + 2 < tiles)
            def _():
                load(t + 2, slot).start()

            return carry

        lax.fori_loop(0, tiles, step, 0)

    def gather(l, j):
        own_rows = xs.at[l, span(d * rows, rows)]
        return remote(own_rows, own_rows, gs.at[l, j], gr.at[l, n - j], peer(j))

    def place(k):
        return group_at(lax.div(k, SPLIT)) * rows + lax.rem(k, SPLIT) * chunk

    def spread(l, k, to, device):
        ref = xd.at[l, span(c * half + place(k), chunk)]
        return remote(ref, ref, zs.at[l, to, k], zr.at[l, k], device)

    def share(l, k):
        ref = xd.at[l, span(c * half + place(k), chunk)]
        return remote(ref, ref, cs.at[l, k], cr.at[l, k], mate)

    def spread_group(l, g):
        for part in range(SPLIT):
            k = g * SPLIT + part

            @pl.when(root)
            def _():
                xd[l, span(c * half + place(k), chunk)] = xs[l, span(place(k), chunk)]

            @pl.when(jnp.logical_not(root))
            def _():
                spread(l, k, 0, down).wait_recv()

            @pl.when(below)
            def _():
                spread(l, k, 0, down).start()

            @pl.when(above)
            def _():
                spread(l, k, 1, up).start()

            share(l, k).start()

    def begin(l):
        for m in range(n):
            j = lax.rem(u + m - d + n, n)

            @pl.when(j != 0)
            def _():
                gather(l, j).start()

        @pl.when(root)
        def _():
            spread_group(l, 0)

    def transpose(p):
        for t in range(0, tiles, n):
            @pl.when(t + p < tiles)
            def _():
                at = span((t + p) * tile, tile)
                t_hi[t + p] = a_hi[at].T
                t_lo[t + p] = a_lo[at].T

    begin(0)
    prepare()

    for l in range(layers):

        def gathered(i):
            rows_of = xs.at[l, span(lax.rem(d + i, n) * rows, rows)]
            return remote(rows_of, rows_of, gs.at[l, i], gr.at[l, i], peer(i))

        def pair(k):
            span_k = span(k * chunk, chunk)
            return remote(swap_out.at[span_k], pair_in.at[l, span_k], ps.at[l, k], pr.at[l, k], mate)

        def chain(k, which):
            span_k = span(k * chunk, chunk)
            return remote(
                own.at[span_k], chain_in.at[l, which, span_k], hs.at[l, k], hr.at[l, which, k], inward
            )

        def total(r):
            return remote(
                own.at[span(r * rows, rows)], total_in.at[l], fs.at[l, r], fr.at[l], {"src": s, "dst": r}
            )

        def reduce_group(i):
            r = group_at(n - 1 - i)
            for part in range(SPLIT):
                k = r * SPLIT + part
                span_k = span(k * chunk, chunk)
                pair(k).wait_recv()
                own[span_k] = own[span_k] + pair_in[l, span_k]

                @pl.when(below)
                def _():
                    chain(k, 0).wait_recv()
                    own[span_k] = own[span_k] + chain_in[l, 0, span_k]

                @pl.when(above)
                def _():
                    chain(k, 1).wait_recv()
                    own[span_k] = own[span_k] + chain_in[l, 1, span_k]

                @pl.when(jnp.logical_not(root))
                def _():
                    chain(k, side).start()

            @pl.when(jnp.logical_and(root, r == d))
            def _():
                total_in[l] = own[span(r * rows, rows)]

            @pl.when(jnp.logical_and(root, r != d))
            def _():
                total(r).start()

        def reverse_out(j):
            rows_of = rev.at[span(lax.rem(d + j, n) * rows, rows)]
            return remote(rows_of, rev_in.at[l, n - j], vs.at[l, j], vr.at[l, n - j], peer(j))

        def reverse():
            def arrive(k, carry):
                share(l, k).wait_recv()
                return carry

            lax.fori_loop(0, chunks, arrive, 0)
            x_hi, x_lo = parts_of(xd[l])
            xd_hi[...] = x_hi
            xd_lo[...] = x_lo

        def reverse_group(i):
            rows_of = span(group_at(n - 1 - i) * rows, rows)
            total_rows = jnp.zeros((rows, width), jnp.float32)
            for t in range(tiles):
                at = pl.ds(t * tile, tile)
                total_rows += dot3(t_hi[t, rows_of], t_lo[t, rows_of], xd_hi[at], xd_lo[at])
            rev[rows_of] = total_rows

            @pl.when(i < n - 1)
            def _():
                reverse_out(offset(n - 1 - i)).start()

        for i in range(1, n):
            gathered(offset(i)).wait_recv()

            @pl.when(root)
            def _():
                spread_group(l, i)

            @pl.when(jnp.logical_and(middle, distance == i))
            def _():
                spread_group(l, 0)

        x_hi, x_lo = parts_of(xs[l])
        xs_hi[...] = x_hi
        xs_lo[...] = x_lo

        def forward(i):
            r = group_at(n - 1 - i)
            start = r * rows
            at = span((1 - c) * half + start, rows)
            swap_out[span(start, rows)] = dot3(a_hi[at], a_lo[at], xs_hi[...], xs_lo[...])
            for part in range(SPLIT):
                pair(r * SPLIT + part).start()
            at = span(c * half + start, rows)
            own[span(start, rows)] = dot3(a_hi[at], a_lo[at], xs_hi[...], xs_lo[...])

        def turn(t, carry):
            @pl.when(t < n)
            def _():
                forward(t)

            if l == 0:
                p = t - jnp.where(tip, n + 1, 0)

                @pl.when(jnp.logical_and(p >= 0, p < n))
                def _():
                    transpose(p)

            @pl.when(t == reverse_turn)
            def _():
                reverse()

            q = t - reverse_turn

            @pl.when(jnp.logical_and(q >= 0, q < n))
            def _():
                reverse_group(q)

            g = t - spread_turn
            first = jnp.where(middle, 1, 0)

            @pl.when(jnp.logical_and(jnp.logical_not(root), jnp.logical_and(g >= first, g < n)))
            def _():
                spread_group(l, g)

            i = t - reduce_turn

            @pl.when(jnp.logical_and(i >= 0, i < n))
            def _():
                reduce_group(i)

            return carry

        lax.fori_loop(0, 3 * n + 1, turn, 0)

        back = rev[span(d * rows, rows)]
        for i in range(1, n):
            remote(
                rev.at[span(d * rows, rows)], rev_in.at[l, i], vs.at[l, i], vr.at[l, i], peer(i)
            ).wait_recv()
            back = back + rev_in[l, i]

        mixed = dot3(*parts_of(back), *parts_of(weights[l, 1])) + biases[pl.ds(l, 1)]

        @pl.when(jnp.logical_not(root))
        def _():
            total(d).wait_recv()

        mixed = mixed + dot3(*parts_of(total_in[l]), *parts_of(weights[l, 0]))
        result = jnp.maximum(mixed, 0.0)
        if l + 1 < layers:
            xs[l + 1, span(d * rows, rows)] = result
            begin(l + 1)
        else:
            out[...] = result

        for j in range(1, n):
            gather(l, j).wait_send()
            reverse_out(j).wait_send()

        def drain(k, carry):
            share(l, k).wait_send()
            pair(k).wait_send()

            @pl.when(below)
            def _():
                spread(l, k, 0, down).wait_send()

            @pl.when(above)
            def _():
                spread(l, k, 1, up).wait_send()

            @pl.when(jnp.logical_not(root))
            def _():
                chain(k, side).wait_send()

            return carry

        lax.fori_loop(0, chunks, drain, 0)
        for r in range(n):

            @pl.when(jnp.logical_and(root, r != d))
            def _():
                total(r).wait_send()


def body(adjacency, features, layer_weights, layer_biases):
    n = lax.axis_size("dst")
    assert lax.axis_size("src") == CORES * n
    layers = layer_weights.shape[0]
    rows, width = features.shape
    half = n * rows
    tile = 256
    tiles = CORES * half // tile
    chunks = n * SPLIT
    f32, bf16 = jnp.float32, jnp.bfloat16
    dma = pltpu.SemaphoreType.DMA
    vmem = pltpu.VMEM
    scratch = [
        vmem((2, tile, half), f32),
        vmem((CORES * half, half), bf16),
        vmem((CORES * half, half), bf16),
        vmem((tiles, half, tile), bf16),
        vmem((tiles, half, tile), bf16),
        vmem((half, width), bf16),
        vmem((half, width), bf16),
        vmem((CORES * half, width), bf16),
        vmem((CORES * half, width), bf16),
        vmem((layers, half, width), f32),
        vmem((layers, CORES * half, width), f32),
        vmem((half, width), f32),
        vmem((half, width), f32),
        vmem((half, width), f32),
        vmem((layers, half, width), f32),
        vmem((layers, 2, half, width), f32),
        vmem((layers, n, rows, width), f32),
        vmem((layers, rows, width), f32),
        dma((2,)),
        dma((layers, n)),
        dma((layers, n)),
        dma((layers, 2, chunks)),
        dma((layers, chunks)),
        dma((layers, chunks)),
        dma((layers, chunks)),
        dma((layers, chunks)),
        dma((layers, chunks)),
        dma((layers, chunks)),
        dma((layers, 2, chunks)),
        dma((layers, n)),
        dma((layers,)),
        dma((layers, n)),
        dma((layers, n)),
    ]
    in_vmem = pl.BlockSpec(memory_space=pltpu.VMEM)
    flops = 2 * 3 * 2 * layers * CORES * half * half * width
    return pl.pallas_call(
        functools.partial(kernel, n, layers, tile),
        out_shape=jax.ShapeDtypeStruct((rows, width), f32),
        in_specs=[pl.BlockSpec(memory_space=pl.ANY), in_vmem, in_vmem, in_vmem],
        out_specs=in_vmem,
        scratch_shapes=scratch,
        compiler_params=pltpu.CompilerParams(
            collective_id=0, has_side_effects=True, vmem_limit_bytes=60 * 2**20
        ),
        cost_estimate=pl.CostEstimate(
            flops=flops, bytes_accessed=adjacency.size * 4, transcendentals=0
        ),
    )(adjacency, features, layer_weights, layer_biases)


def solution(mesh):
    placed = (P("dst", "src"), P(("src", "dst"), None), P(), P())
    return jax.shard_map(
        body, mesh=mesh, in_specs=placed, out_specs=P(("src", "dst"), None), check_vma=False
    )
```

```python
import functools

import jax
import jax.numpy as jnp
from jax import lax
from jax.experimental import pallas as pl
from jax.experimental.pallas import tpu as pltpu
from jax.sharding import PartitionSpec as P

MESH = pl.DeviceIdType.MESH
CORES = 2
SPLIT = 2


def parts_of(value):
    high = value.astype(jnp.bfloat16)
    return high, (value - high.astype(jnp.float32)).astype(jnp.bfloat16)


def dot3(a_high, a_low, b_high, b_low):
    dot = functools.partial(jnp.dot, preferred_element_type=jnp.float32)
    return dot(a_high, b_high) + (dot(a_high, b_low) + dot(a_low, b_high))


def kernel(
    n, layers, tile,
    adj, feat, weights, biases, out,
    stage, a_hi, a_lo, t_hi, t_lo, xs_hi, xs_lo, xd_hi, xd_lo,
    xs, xd, swap_out, own, rev, pair_in, chain_in, rev_in, total_in,
    load_sem, gs, gr, zs, zr, cs, cr, ps, pr, hs, hr, fs, fr, vs, vr,
):
    rows, width = feat.shape
    half = n * rows
    chunk = rows // SPLIT
    chunks = n * SPLIT
    tiles = CORES * half // tile
    s, d = lax.axis_index("src"), lax.axis_index("dst")
    u, c = lax.div(s, CORES), lax.rem(s, CORES)
    root = u == d
    below = jnp.logical_and(u <= d, u > 0)
    above = jnp.logical_and(u >= d, u < n - 1)
    distance = jnp.abs(u - d)
    reach = jnp.where(u < d, d, n - 1 - d)
    tip = jnp.logical_and(jnp.logical_not(root), distance == reach)
    middle = jnp.logical_not(jnp.logical_or(root, tip))
    reverse_turn = jnp.where(tip, 2 * n + 1, n)
    spread_turn = jnp.where(tip, n + 1, -1)
    reduce_turn = jnp.where(root, 2 * n - 1, jnp.where(tip, 1, 1 + reach - distance))
    mate = {"src": u * CORES + 1 - c, "dst": d}
    down = {"src": s - CORES, "dst": d}
    up = {"src": s + CORES, "dst": d}
    inward = {"src": jnp.where(u < d, s + CORES, s - CORES), "dst": d}
    side = jnp.where(u < d, 0, 1)

    def offset(i):
        return lax.rem(jnp.where(d < n // 2, i, n - i), n)

    def group_at(i):
        return lax.rem(d + offset(i), n)

    def peer(j):
        return {"src": s, "dst": lax.rem(d + j, n)}

    def span(start, size):
        return pl.ds(pl.multiple_of(start, size), size)

    def remote(src, dst, send, recv, device):
        return pltpu.make_async_remote_copy(
            src_ref=src, dst_ref=dst, send_sem=send, recv_sem=recv,
            device_id=device, device_id_type=MESH,
        )

    def load(t, slot):
        return pltpu.make_async_copy(adj.at[span(t * tile, tile)], stage.at[slot], load_sem.at[slot])

    load(0, 0).start()
    if tiles > 1:
        load(1, 1).start()

    barrier = pltpu.get_barrier_semaphore()
    for j in range(1, n):
        pl.semaphore_signal(barrier, inc=1, device_id=peer(j), device_id_type=MESH)
    pl.semaphore_signal(barrier, inc=1, device_id=mate, device_id_type=MESH)

    @pl.when(u > 0)
    def _():
        pl.semaphore_signal(barrier, inc=1, device_id=down, device_id_type=MESH)

    @pl.when(u < n - 1)
    def _():
        pl.semaphore_signal(barrier, inc=1, device_id=up, device_id_type=MESH)

    xs[0, span(d * rows, rows)] = feat[...]
    pl.semaphore_wait(barrier, n + (u > 0).astype(jnp.int32) + (u < n - 1).astype(jnp.int32))

    def prepare():
        def step(t, carry):
            slot = lax.rem(t, 2)
            load(t, slot).wait()
            block = stage[slot]
            high, low = parts_of(block)
            a_hi[span(t * tile, tile)] = high
            a_lo[span(t * tile, tile)] = low
            turned_high, turned_low = parts_of(block.T)
            t_hi[t] = turned_high
            t_lo[t] = turned_low

            @pl.when(t + 2 < tiles)
            def _():
                load(t + 2, slot).start()

            return carry

        lax.fori_loop(0, tiles, step, 0)

    def gather(l, j):
        own_rows = xs.at[l, span(d * rows, rows)]
        return remote(own_rows, own_rows, gs.at[l, j], gr.at[l, n - j], peer(j))

    def place(k):
        return group_at(lax.div(k, SPLIT)) * rows + lax.rem(k, SPLIT) * chunk

    def spread(l, k, to, device):
        ref = xd.at[l, span(c * half + place(k), chunk)]
        return remote(ref, ref, zs.at[l, to, k], zr.at[l, k], device)

    def share(l, k):
        ref = xd.at[l, span(c * half + place(k), chunk)]
        return remote(ref, ref, cs.at[l, k], cr.at[l, k], mate)

    def spread_group(l, g):
        for part in range(SPLIT):
            k = g * SPLIT + part

            @pl.when(root)
            def _():
                xd[l, span(c * half + place(k), chunk)] = xs[l, span(place(k), chunk)]

            @pl.when(jnp.logical_not(root))
            def _():
                spread(l, k, 0, down).wait_recv()

            @pl.when(below)
            def _():
                spread(l, k, 0, down).start()

            @pl.when(above)
            def _():
                spread(l, k, 1, up).start()

            share(l, k).start()

    def begin(l):
        for m in range(n):
            j = lax.rem(u + m - d + n, n)

            @pl.when(j != 0)
            def _():
                gather(l, j).start()

        @pl.when(root)
        def _():
            spread_group(l, 0)

    begin(0)
    prepare()

    for l in range(layers):

        def gathered(i):
            rows_of = xs.at[l, span(lax.rem(d + i, n) * rows, rows)]
            return remote(rows_of, rows_of, gs.at[l, i], gr.at[l, i], peer(i))

        def pair(k):
            span_k = span(k * chunk, chunk)
            return remote(swap_out.at[span_k], pair_in.at[l, span_k], ps.at[l, k], pr.at[l, k], mate)

        def chain(k, which):
            span_k = span(k * chunk, chunk)
            return remote(
                own.at[span_k], chain_in.at[l, which, span_k], hs.at[l, k], hr.at[l, which, k], inward
            )

        def total(r):
            return remote(
                own.at[span(r * rows, rows)], total_in.at[l], fs.at[l, r], fr.at[l], {"src": s, "dst": r}
            )

        def reduce_group(i):
            r = group_at(n - 1 - i)
            for part in range(SPLIT):
                k = r * SPLIT + part
                span_k = span(k * chunk, chunk)
                pair(k).wait_recv()
                own[span_k] = own[span_k] + pair_in[l, span_k]

                @pl.when(below)
                def _():
                    chain(k, 0).wait_recv()
                    own[span_k] = own[span_k] + chain_in[l, 0, span_k]

                @pl.when(above)
                def _():
                    chain(k, 1).wait_recv()
                    own[span_k] = own[span_k] + chain_in[l, 1, span_k]

                @pl.when(jnp.logical_not(root))
                def _():
                    chain(k, side).start()

            @pl.when(jnp.logical_and(root, r == d))
            def _():
                total_in[l] = own[span(r * rows, rows)]

            @pl.when(jnp.logical_and(root, r != d))
            def _():
                total(r).start()

        def reverse_out(j):
            rows_of = rev.at[span(lax.rem(d + j, n) * rows, rows)]
            return remote(rows_of, rev_in.at[l, n - j], vs.at[l, j], vr.at[l, n - j], peer(j))

        def reverse():
            def arrive(k, carry):
                share(l, k).wait_recv()
                return carry

            lax.fori_loop(0, chunks, arrive, 0)
            x_hi, x_lo = parts_of(xd[l])
            xd_hi[...] = x_hi
            xd_lo[...] = x_lo

        def reverse_group(i):
            rows_of = span(group_at(n - 1 - i) * rows, rows)
            total_rows = jnp.zeros((rows, width), jnp.float32)
            for t in range(tiles):
                at = pl.ds(t * tile, tile)
                total_rows += dot3(t_hi[t, rows_of], t_lo[t, rows_of], xd_hi[at], xd_lo[at])
            rev[rows_of] = total_rows

            @pl.when(i < n - 1)
            def _():
                reverse_out(offset(n - 1 - i)).start()

        for i in range(1, n):
            gathered(offset(i)).wait_recv()

            @pl.when(root)
            def _():
                spread_group(l, i)

            @pl.when(jnp.logical_and(middle, distance == i))
            def _():
                spread_group(l, 0)

        x_hi, x_lo = parts_of(xs[l])
        xs_hi[...] = x_hi
        xs_lo[...] = x_lo

        def forward(i):
            r = group_at(n - 1 - i)
            start = r * rows
            at = span((1 - c) * half + start, rows)
            swap_out[span(start, rows)] = dot3(a_hi[at], a_lo[at], xs_hi[...], xs_lo[...])
            for part in range(SPLIT):
                pair(r * SPLIT + part).start()
            at = span(c * half + start, rows)
            own[span(start, rows)] = dot3(a_hi[at], a_lo[at], xs_hi[...], xs_lo[...])

        def turn(t, carry):
            @pl.when(t < n)
            def _():
                forward(t)

            @pl.when(t == reverse_turn)
            def _():
                reverse()

            q = t - reverse_turn

            @pl.when(jnp.logical_and(q >= 0, q < n))
            def _():
                reverse_group(q)

            g = t - spread_turn
            first = jnp.where(middle, 1, 0)

            @pl.when(jnp.logical_and(jnp.logical_not(root), jnp.logical_and(g >= first, g < n)))
            def _():
                spread_group(l, g)

            i = t - reduce_turn

            @pl.when(jnp.logical_and(i >= 0, i < n))
            def _():
                reduce_group(i)

            return carry

        lax.fori_loop(0, 3 * n + 1, turn, 0)

        back = rev[span(d * rows, rows)]
        for i in range(1, n):
            remote(
                rev.at[span(d * rows, rows)], rev_in.at[l, i], vs.at[l, i], vr.at[l, i], peer(i)
            ).wait_recv()
            back = back + rev_in[l, i]

        mixed = dot3(*parts_of(back), *parts_of(weights[l, 1])) + biases[pl.ds(l, 1)]

        @pl.when(jnp.logical_not(root))
        def _():
            total(d).wait_recv()

        mixed = mixed + dot3(*parts_of(total_in[l]), *parts_of(weights[l, 0]))
        result = jnp.maximum(mixed, 0.0)
        if l + 1 < layers:
            xs[l + 1, span(d * rows, rows)] = result
            begin(l + 1)
        else:
            out[...] = result

        for j in range(1, n):
            gather(l, j).wait_send()
            reverse_out(j).wait_send()

        def drain(k, carry):
            share(l, k).wait_send()
            pair(k).wait_send()

            @pl.when(below)
            def _():
                spread(l, k, 0, down).wait_send()

            @pl.when(above)
            def _():
                spread(l, k, 1, up).wait_send()

            @pl.when(jnp.logical_not(root))
            def _():
                chain(k, side).wait_send()

            return carry

        lax.fori_loop(0, chunks, drain, 0)
        for r in range(n):

            @pl.when(jnp.logical_and(root, r != d))
            def _():
                total(r).wait_send()


def body(adjacency, features, layer_weights, layer_biases):
    n = lax.axis_size("dst")
    assert lax.axis_size("src") == CORES * n
    layers = layer_weights.shape[0]
    rows, width = features.shape
    half = n * rows
    tile = 256
    tiles = CORES * half // tile
    chunks = n * SPLIT
    f32, bf16 = jnp.float32, jnp.bfloat16
    dma = pltpu.SemaphoreType.DMA
    vmem = pltpu.VMEM
    scratch = [
        vmem((2, tile, half), f32),
        vmem((CORES * half, half), bf16),
        vmem((CORES * half, half), bf16),
        vmem((tiles, half, tile), bf16),
        vmem((tiles, half, tile), bf16),
        vmem((half, width), bf16),
        vmem((half, width), bf16),
        vmem((CORES * half, width), bf16),
        vmem((CORES * half, width), bf16),
        vmem((layers, half, width), f32),
        vmem((layers, CORES * half, width), f32),
        vmem((half, width), f32),
        vmem((half, width), f32),
        vmem((half, width), f32),
        vmem((layers, half, width), f32),
        vmem((layers, 2, half, width), f32),
        vmem((layers, n, rows, width), f32),
        vmem((layers, rows, width), f32),
        dma((2,)),
        dma((layers, n)),
        dma((layers, n)),
        dma((layers, 2, chunks)),
        dma((layers, chunks)),
        dma((layers, chunks)),
        dma((layers, chunks)),
        dma((layers, chunks)),
        dma((layers, chunks)),
        dma((layers, chunks)),
        dma((layers, 2, chunks)),
        dma((layers, n)),
        dma((layers,)),
        dma((layers, n)),
        dma((layers, n)),
    ]
    in_vmem = pl.BlockSpec(memory_space=pltpu.VMEM)
    flops = 2 * 3 * 2 * layers * CORES * half * half * width
    return pl.pallas_call(
        functools.partial(kernel, n, layers, tile),
        out_shape=jax.ShapeDtypeStruct((rows, width), f32),
        in_specs=[pl.BlockSpec(memory_space=pl.ANY), in_vmem, in_vmem, in_vmem],
        out_specs=in_vmem,
        scratch_shapes=scratch,
        compiler_params=pltpu.CompilerParams(
            collective_id=0, has_side_effects=True, vmem_limit_bytes=60 * 2**20
        ),
        cost_estimate=pl.CostEstimate(
            flops=flops, bytes_accessed=adjacency.size * 4, transcendentals=0
        ),
    )(adjacency, features, layer_weights, layer_biases)


def solution(mesh):
    placed = (P("dst", "src"), P(("src", "dst"), None), P(), P())
    return jax.shard_map(
        body, mesh=mesh, in_specs=placed, out_specs=P(("src", "dst"), None), check_vma=False
    )
```

```python
import functools

import jax
import jax.numpy as jnp
from jax import lax
from jax.experimental import pallas as pl
from jax.experimental.pallas import tpu as pltpu
from jax.sharding import PartitionSpec as P

MESH = pl.DeviceIdType.MESH
CORES = 2
SPLIT = 2


def parts_of(value):
    high = value.astype(jnp.bfloat16)
    return high, (value - high.astype(jnp.float32)).astype(jnp.bfloat16)


def dot3(a_high, a_low, b_high, b_low):
    dot = functools.partial(jnp.dot, preferred_element_type=jnp.float32)
    return dot(a_high, b_high) + (dot(a_high, b_low) + dot(a_low, b_high))


def kernel(
    n, layers, tile,
    adj, feat, weights, biases, out,
    stage, a_hi, a_lo, t_hi, t_lo, xs_hi, xs_lo, xd_hi, xd_lo,
    xs, xd, swap_out, own, rev, pair_in, chain_in, rev_in, total_in,
    load_sem, gs, gr, zs, zr, cs, cr, ps, pr, hs, hr, fs, fr, vs, vr,
):
    rows, width = feat.shape
    half = n * rows
    chunk = rows // SPLIT
    chunks = n * SPLIT
    tiles = CORES * half // tile
    s, d = lax.axis_index("src"), lax.axis_index("dst")
    u, c = lax.div(s, CORES), lax.rem(s, CORES)
    root = u == d
    below = jnp.logical_and(u <= d, u > 0)
    above = jnp.logical_and(u >= d, u < n - 1)
    distance = jnp.abs(u - d)
    reach = jnp.where(u < d, d, n - 1 - d)
    tip = jnp.logical_and(jnp.logical_not(root), distance == reach)
    middle = jnp.logical_not(jnp.logical_or(root, tip))
    reverse_turn = jnp.where(tip, 2 * n + 1, jnp.where(middle, n + 1, n))
    spread_turn = jnp.where(tip, n + 1, jnp.where(middle, 1, 0))
    reduce_turn = jnp.where(root, 2 * n - 1, jnp.where(tip, 1, 1 + reach - distance))
    mate = {"src": u * CORES + 1 - c, "dst": d}
    down = {"src": s - CORES, "dst": d}
    up = {"src": s + CORES, "dst": d}
    inward = {"src": jnp.where(u < d, s + CORES, s - CORES), "dst": d}
    side = jnp.where(u < d, 0, 1)

    def offset(i):
        return lax.rem(jnp.where(d < n // 2, i, n - i), n)

    def group_at(i):
        return lax.rem(d + offset(i), n)

    def peer(j):
        return {"src": s, "dst": lax.rem(d + j, n)}

    def span(start, size):
        return pl.ds(pl.multiple_of(start, size), size)

    def remote(src, dst, send, recv, device):
        return pltpu.make_async_remote_copy(
            src_ref=src, dst_ref=dst, send_sem=send, recv_sem=recv,
            device_id=device, device_id_type=MESH,
        )

    def load(t, slot):
        return pltpu.make_async_copy(adj.at[span(t * tile, tile)], stage.at[slot], load_sem.at[slot])

    load(0, 0).start()
    if tiles > 1:
        load(1, 1).start()

    barrier = pltpu.get_barrier_semaphore()
    for j in range(1, n):
        pl.semaphore_signal(barrier, inc=1, device_id=peer(j), device_id_type=MESH)
    pl.semaphore_signal(barrier, inc=1, device_id=mate, device_id_type=MESH)

    @pl.when(u > 0)
    def _():
        pl.semaphore_signal(barrier, inc=1, device_id=down, device_id_type=MESH)

    @pl.when(u < n - 1)
    def _():
        pl.semaphore_signal(barrier, inc=1, device_id=up, device_id_type=MESH)

    xs[0, span(d * rows, rows)] = feat[...]
    pl.semaphore_wait(barrier, n + (u > 0).astype(jnp.int32) + (u < n - 1).astype(jnp.int32))

    def prepare():
        def step(t, carry):
            slot = lax.rem(t, 2)
            load(t, slot).wait()
            block = stage[slot]
            high, low = parts_of(block)
            a_hi[span(t * tile, tile)] = high
            a_lo[span(t * tile, tile)] = low
            turned_high, turned_low = parts_of(block.T)
            t_hi[t] = turned_high
            t_lo[t] = turned_low

            @pl.when(t + 2 < tiles)
            def _():
                load(t + 2, slot).start()

            return carry

        lax.fori_loop(0, tiles, step, 0)

    def gather(l, j):
        own_rows = xs.at[l, span(d * rows, rows)]
        return remote(own_rows, own_rows, gs.at[l, j], gr.at[l, n - j], peer(j))

    def place(k):
        return group_at(lax.div(k, SPLIT)) * rows + lax.rem(k, SPLIT) * chunk

    def spread(l, k, to, device):
        ref = xd.at[l, span(c * half + place(k), chunk)]
        return remote(ref, ref, zs.at[l, to, k], zr.at[l, k], device)

    def share(l, k):
        ref = xd.at[l, span(c * half + place(k), chunk)]
        return remote(ref, ref, cs.at[l, k], cr.at[l, k], mate)

    def spread_group(l, g):
        for part in range(SPLIT):
            k = g * SPLIT + part

            @pl.when(root)
            def _():
                xd[l, span(c * half + place(k), chunk)] = xs[l, span(place(k), chunk)]

            @pl.when(jnp.logical_not(root))
            def _():
                spread(l, k, 0, down).wait_recv()

            @pl.when(below)
            def _():
                spread(l, k, 0, down).start()

            @pl.when(above)
            def _():
                spread(l, k, 1, up).start()

            share(l, k).start()

    def begin(l):
        for m in range(n):
            j = lax.rem(u + m - d + n, n)

            @pl.when(j != 0)
            def _():
                gather(l, j).start()

        @pl.when(root)
        def _():
            spread_group(l, 0)

    begin(0)
    prepare()

    for l in range(layers):

        def gathered(i):
            rows_of = xs.at[l, span(lax.rem(d + i, n) * rows, rows)]
            return remote(rows_of, rows_of, gs.at[l, i], gr.at[l, i], peer(i))

        def pair(k):
            span_k = span(k * chunk, chunk)
            return remote(swap_out.at[span_k], pair_in.at[l, span_k], ps.at[l, k], pr.at[l, k], mate)

        def chain(k, which):
            span_k = span(k * chunk, chunk)
            return remote(
                own.at[span_k], chain_in.at[l, which, span_k], hs.at[l, k], hr.at[l, which, k], inward
            )

        def total(r):
            return remote(
                own.at[span(r * rows, rows)], total_in.at[l], fs.at[l, r], fr.at[l], {"src": s, "dst": r}
            )

        def reduce_group(i):
            r = group_at(n - 1 - i)
            for part in range(SPLIT):
                k = r * SPLIT + part
                span_k = span(k * chunk, chunk)
                pair(k).wait_recv()
                own[span_k] = own[span_k] + pair_in[l, span_k]

                @pl.when(below)
                def _():
                    chain(k, 0).wait_recv()
                    own[span_k] = own[span_k] + chain_in[l, 0, span_k]

                @pl.when(above)
                def _():
                    chain(k, 1).wait_recv()
                    own[span_k] = own[span_k] + chain_in[l, 1, span_k]

                @pl.when(jnp.logical_not(root))
                def _():
                    chain(k, side).start()

            @pl.when(jnp.logical_and(root, r == d))
            def _():
                total_in[l] = own[span(r * rows, rows)]

            @pl.when(jnp.logical_and(root, r != d))
            def _():
                total(r).start()

        def reverse_out(j):
            rows_of = rev.at[span(lax.rem(d + j, n) * rows, rows)]
            return remote(rows_of, rev_in.at[l, n - j], vs.at[l, j], vr.at[l, n - j], peer(j))

        def reverse():
            def arrive(k, carry):
                share(l, k).wait_recv()
                return carry

            lax.fori_loop(0, chunks, arrive, 0)
            x_hi, x_lo = parts_of(xd[l])
            xd_hi[...] = x_hi
            xd_lo[...] = x_lo

        def reverse_group(i):
            rows_of = span(group_at(n - 1 - i) * rows, rows)
            total_rows = jnp.zeros((rows, width), jnp.float32)
            for t in range(tiles):
                at = pl.ds(t * tile, tile)
                total_rows += dot3(t_hi[t, rows_of], t_lo[t, rows_of], xd_hi[at], xd_lo[at])
            rev[rows_of] = total_rows

            @pl.when(i < n - 1)
            def _():
                reverse_out(offset(n - 1 - i)).start()

        for i in range(1, n):
            gathered(offset(i)).wait_recv()

            @pl.when(root)
            def _():
                spread_group(l, i)

            @pl.when(jnp.logical_and(middle, distance == i))
            def _():
                spread_group(l, 0)

        x_hi, x_lo = parts_of(xs[l])
        xs_hi[...] = x_hi
        xs_lo[...] = x_lo

        def forward(i):
            r = group_at(n - 1 - i)
            start = r * rows
            at = span((1 - c) * half + start, rows)
            swap_out[span(start, rows)] = dot3(a_hi[at], a_lo[at], xs_hi[...], xs_lo[...])
            for part in range(SPLIT):
                pair(r * SPLIT + part).start()
            at = span(c * half + start, rows)
            own[span(start, rows)] = dot3(a_hi[at], a_lo[at], xs_hi[...], xs_lo[...])

        def turn(t, carry):
            @pl.when(t < n)
            def _():
                forward(t)

            @pl.when(t == reverse_turn)
            def _():
                reverse()

            q = t - reverse_turn

            @pl.when(jnp.logical_and(q >= 0, q < n))
            def _():
                reverse_group(q)

            g = t - spread_turn
            first = jnp.where(middle, 1, 0)

            @pl.when(jnp.logical_and(jnp.logical_not(root), jnp.logical_and(g >= first, g < n)))
            def _():
                spread_group(l, g)

            i = t - reduce_turn

            @pl.when(jnp.logical_and(i >= 0, i < n))
            def _():
                reduce_group(i)

            return carry

        lax.fori_loop(0, 3 * n + 1, turn, 0)

        back = rev[span(d * rows, rows)]
        for i in range(1, n):
            remote(
                rev.at[span(d * rows, rows)], rev_in.at[l, i], vs.at[l, i], vr.at[l, i], peer(i)
            ).wait_recv()
            back = back + rev_in[l, i]

        mixed = dot3(*parts_of(back), *parts_of(weights[l, 1])) + biases[pl.ds(l, 1)]

        @pl.when(jnp.logical_not(root))
        def _():
            total(d).wait_recv()

        mixed = mixed + dot3(*parts_of(total_in[l]), *parts_of(weights[l, 0]))
        result = jnp.maximum(mixed, 0.0)
        if l + 1 < layers:
            xs[l + 1, span(d * rows, rows)] = result
            begin(l + 1)
        else:
            out[...] = result

        for j in range(1, n):
            gather(l, j).wait_send()
            reverse_out(j).wait_send()

        def drain(k, carry):
            share(l, k).wait_send()
            pair(k).wait_send()

            @pl.when(below)
            def _():
                spread(l, k, 0, down).wait_send()

            @pl.when(above)
            def _():
                spread(l, k, 1, up).wait_send()

            @pl.when(jnp.logical_not(root))
            def _():
                chain(k, side).wait_send()

            return carry

        lax.fori_loop(0, chunks, drain, 0)
        for r in range(n):

            @pl.when(jnp.logical_and(root, r != d))
            def _():
                total(r).wait_send()


def body(adjacency, features, layer_weights, layer_biases):
    n = lax.axis_size("dst")
    assert lax.axis_size("src") == CORES * n
    layers = layer_weights.shape[0]
    rows, width = features.shape
    half = n * rows
    tile = 256
    tiles = CORES * half // tile
    chunks = n * SPLIT
    f32, bf16 = jnp.float32, jnp.bfloat16
    dma = pltpu.SemaphoreType.DMA
    vmem = pltpu.VMEM
    scratch = [
        vmem((2, tile, half), f32),
        vmem((CORES * half, half), bf16),
        vmem((CORES * half, half), bf16),
        vmem((tiles, half, tile), bf16),
        vmem((tiles, half, tile), bf16),
        vmem((half, width), bf16),
        vmem((half, width), bf16),
        vmem((CORES * half, width), bf16),
        vmem((CORES * half, width), bf16),
        vmem((layers, half, width), f32),
        vmem((layers, CORES * half, width), f32),
        vmem((half, width), f32),
        vmem((half, width), f32),
        vmem((half, width), f32),
        vmem((layers, half, width), f32),
        vmem((layers, 2, half, width), f32),
        vmem((layers, n, rows, width), f32),
        vmem((layers, rows, width), f32),
        dma((2,)),
        dma((layers, n)),
        dma((layers, n)),
        dma((layers, 2, chunks)),
        dma((layers, chunks)),
        dma((layers, chunks)),
        dma((layers, chunks)),
        dma((layers, chunks)),
        dma((layers, chunks)),
        dma((layers, chunks)),
        dma((layers, 2, chunks)),
        dma((layers, n)),
        dma((layers,)),
        dma((layers, n)),
        dma((layers, n)),
    ]
    in_vmem = pl.BlockSpec(memory_space=pltpu.VMEM)
    flops = 2 * 3 * 2 * layers * CORES * half * half * width
    return pl.pallas_call(
        functools.partial(kernel, n, layers, tile),
        out_shape=jax.ShapeDtypeStruct((rows, width), f32),
        in_specs=[pl.BlockSpec(memory_space=pl.ANY), in_vmem, in_vmem, in_vmem],
        out_specs=in_vmem,
        scratch_shapes=scratch,
        compiler_params=pltpu.CompilerParams(
            collective_id=0, has_side_effects=True, vmem_limit_bytes=60 * 2**20
        ),
        cost_estimate=pl.CostEstimate(
            flops=flops, bytes_accessed=adjacency.size * 4, transcendentals=0
        ),
    )(adjacency, features, layer_weights, layer_biases)


def solution(mesh):
    placed = (P("dst", "src"), P(("src", "dst"), None), P(), P())
    return jax.shard_map(
        body, mesh=mesh, in_specs=placed, out_specs=P(("src", "dst"), None), check_vma=False
    )
```
